128 devices in a mesh: node: 32 (over z, y, x_lo), local: 2 (over core), section: 2 (over x_hi).
Axes of the slice: x: 4 (x_hi: 2, x_lo: 2; x = x_hi * 2 + x_lo), y: 4, z: 4, core: 2. Of those that a mesh axis runs over, the one named last changes fastest.
Arguments:
- tokens: bfloat16 [2, 4096, 4096], P('section', 'node', 'local'), may hold values from -6 to 6
- expert_ids: int32 [2, 4096, 8], P('section', 'node'), may hold values from 0 to 31, all different within a row; in each aligned block of 128 rows (0 to 127, 128 to 255, ..., all dimensions but the last counted through in order) at most 64 rows name the same one
- gate_weights: float32 [2, 4096, 8], P('section', 'node'), may hold values from 0.1 to 1
- expert_node: int32 [2, 32], P('section'), may hold values from 0 to 31, each once within a row
- w_gate: bfloat16 [2, 32, 4096, 1024], P('section', 'node', None, 'local'), may hold values from -0.09375 to 0.09375
- w_up: bfloat16 [2, 32, 4096, 1024], P('section', 'node', None, 'local'), may hold values from -0.09375 to 0.09375
- w_down: bfloat16 [2, 32, 1024, 4096], P('section', 'node', 'local'), may hold values from -0.25 to 0.25
Outputs:
- mixed: bfloat16 [2, 4096, 4096], P('section', 'node', 'local')
The draws below stay inside these ranges and needn't reach their ends.
Inputs may be any that keep to these rules, and one draw needn't show every extreme that they name: `expert_ids`: in each block of 128 rows of one segment (the rows of one node index) no expert is chosen by more than 64 rows, a bound that some block reaches; the 8 experts of a token differ. `expert_node`: each segment's row names every node index once.
All inputs are finite; a program needn't handle non-finite values.
Results may differ from the reference program's by a relative error of at most 0.0061.
Values may be sent and summed in bfloat16 or wider, within the bound.
A program may use at most 128 MiB of HBM per device.

```python
import math
import jax
import jax.numpy as jnp
import numpy as np

D = 4096
FFE = 1024
TOPK = 8
TOK_DEV = 128
CAP = 64
EXPERTS = 32
TOKENS = 4096
N_NODE = 32
N_LOCAL = 2
N_SECTION = 2


def spiked(drawn, own_key, source, target, shards_of, factor):
    owner, partner = [(jnp.arange(drawn.shape[position]) // (drawn.shape[position] // shards_of)).reshape([-1 if axis == position else 1 for axis in range(drawn.ndim)]) for position in (source, target)]
    chosen = jax.random.permutation(own_key, shards_of)[partner]
    strong = (owner == chosen) | (owner == (partner + shards_of // 2) % shards_of)
    return jnp.where(strong, factor * drawn, drawn)


def shard_levels(stream_key, shape, cuts, low, top_value):
    def one(dim, blocks):
        draws = jax.random.uniform(jax.random.fold_in(jax.random.fold_in(stream_key, 6), dim), (blocks,), jnp.float32, low / len(cuts), top_value / len(cuts))
        return jnp.repeat(jnp.exp(draws), shape[dim] // blocks).reshape((-1,) + (1,) * (len(shape) - dim - 1))

    gain = one(*cuts[0])
    for cut in cuts[1:]:
        gain = gain * one(*cut)
    return gain


def deal_out(stream_key, own, number, rows, amount, top, bound, skew):
    sequence = jax.random.permutation(stream_key, amount)
    heavy_load, ordinary = load_shares(amount, rows * top, bound, skew, True), load_shares(amount, rows * top, bound, skew, False)
    places = jnp.arange(amount)

    def named(lengths, turn):
        used = int((lengths > 0).sum())
        fixed = max(1, used // 4)
        shifted = fixed + (places - fixed + turn * (used - fixed)) % max(1, amount - fixed)
        return jnp.zeros((amount,), jnp.int32).at[sequence[jnp.where(places < fixed, places, shifted)]].set(jnp.asarray(lengths, jnp.int32))

    lengths = jnp.where(number % 4 == 0, named(heavy_load, number // 4), named(ordinary, number - number // 4 - 1))
    mixed = jax.random.permutation(jax.random.fold_in(own, 3), amount)
    donor, taker = mixed[0:amount // 2 * 2:2], mixed[1:amount // 2 * 2:2]
    slack = jnp.minimum(lengths[donor] - 1, bound - lengths[taker]) // 2
    slack = jnp.where((donor == sequence[0]) | (taker == sequence[0]) | (lengths[taker] == 0), 0, jnp.maximum(slack, 0))
    shifted = jax.random.randint(jax.random.fold_in(own, 4), (amount // 2,), 0, 1 << 20) % (slack + 1)
    lengths = lengths.at[donor].add(-shifted).at[taker].add(shifted)
    members = jnp.searchsorted(jnp.cumsum(lengths), jnp.arange(rows * top), side="right").astype(jnp.int32)
    listing = members.reshape(top, rows).T
    listing = listing[jax.random.permutation(jax.random.fold_in(own, 1), rows)]
    turn = jax.random.randint(jax.random.fold_in(own, 2), (rows, 1), 0, top)
    return jnp.take_along_axis(listing, (jnp.arange(top)[None, :] + turn) % top, axis=1)


def load_shares(amount, total, most, lean, full):
    portions = [(1 << 20) // math.isqrt(standing ** lean) + 1 for standing in range(1, amount + 1)]
    largest = most if full else min(most, max(-(-total // amount), total * portions[0] // sum(portions)))
    least = 1 if total - largest >= amount - 1 else 0
    counts, rest = [largest] + [least] * (amount - 1), total - largest - least * (amount - 1)
    while rest > 0:
        candidates = [i for i in range(1, amount) if counts[i] < largest] or [i for i in range(1, amount) if counts[i] < most]
        pool, left = sum([portions[i] for i in candidates]), rest
        for i in candidates:
            more = min(most - counts[i], max(1, left * portions[i] // pool), rest)
            counts[i] = counts[i] + more
            rest = rest - more
    return np.array(counts)


def scatter_about(stream_key, dims, width, bound, cuts=(), kind=jnp.bfloat16):
    array = width * jax.random.normal(stream_key, dims, jnp.float32)
    if cuts:
        array = array * shard_levels(stream_key, dims, cuts, -0.22, 0.18)
    return jnp.clip(array, -bound, bound).astype(kind)


def gaussian_with(rng, shape, deviation, limit, pieces, heavy, kind=jnp.bfloat16):
    entries = deviation * jax.random.normal(rng, shape, jnp.float32)
    if pieces:
        entries = entries * shard_levels(rng, shape, pieces, -0.22, 0.18)
    return jnp.clip(spiked(entries, jax.random.fold_in(rng, 3), *heavy), -limit, limit).astype(kind)


def setup_inputs(seed: int = 0) -> dict:
    streams_of = jax.random.split(jax.random.key(seed), 8)
    tokens = scatter_about(streams_of[0], (N_SECTION, TOKENS, D), 1.0, 6.0, ((0, 2), (1, 32), (2, 2)))
    expert_ids_keys = jax.random.split(jax.random.fold_in(streams_of[1], 1), N_SECTION * TOKENS // TOK_DEV)
    expert_ids_turns = jax.random.permutation(jax.random.fold_in(streams_of[1], 3), N_SECTION * TOKENS // TOK_DEV)
    expert_ids = jax.vmap(lambda own, number: deal_out(jax.random.fold_in(streams_of[1], 2), own, number, TOK_DEV, EXPERTS, TOPK, CAP, 2))(expert_ids_keys, expert_ids_turns).reshape((N_SECTION, TOKENS, TOPK))
    gate_weights = jnp.clip(jnp.exp(math.log(1.0) - 2.3025851 * jax.random.uniform(streams_of[2], (N_SECTION, TOKENS, TOPK), jnp.float32) ** shard_levels(streams_of[2], (N_SECTION, TOKENS, TOPK), ((0, 2), (1, 32)), -0.2, 0.2)), 0.1, 1.0)
    expert_node = jax.vmap(lambda own: jax.random.permutation(own, EXPERTS))(jax.random.split(streams_of[3], N_SECTION)).reshape((N_SECTION, EXPERTS)).astype(jnp.int32)
    w_gate = scatter_about(streams_of[4], (N_SECTION, EXPERTS, D, FFE), D ** -0.5, 0.09375, ((0, 2), (1, 32), (3, 2)))
    w_up = scatter_about(streams_of[5], (N_SECTION, EXPERTS, D, FFE), D ** -0.5, 0.09375, ((0, 2), (1, 32), (3, 2)))
    w_down = gaussian_with(streams_of[6], (N_SECTION, EXPERTS, FFE, D), FFE ** -0.5, 0.25, ((0, 2), (1, 32), (2, 2)), (2, 3, 2, 2.0))
    return dict(tokens=tokens, expert_ids=expert_ids, gate_weights=gate_weights, expert_node=expert_node, w_gate=w_gate, w_up=w_up, w_down=w_down)


def segment_layer(tok, ids, gates, placed, wg, wu, wd):
    pairs = TOK_DEV * TOPK
    flat = ids.reshape(N_NODE, pairs)
    onehot = (flat[:, :, None] == jnp.arange(EXPERTS, dtype=jnp.int32)[None, None, :]).astype(jnp.int32)
    slot = jnp.sum((jnp.cumsum(onehot, axis=1) - 1) * onehot, axis=2).astype(jnp.int32)
    home = placed[flat].astype(jnp.int32)
    source = jnp.broadcast_to(jnp.arange(N_NODE, dtype=jnp.int32)[:, None], (N_NODE, pairs))
    local_row = jnp.broadcast_to((jnp.arange(pairs, dtype=jnp.int32) // TOPK)[None, :], (N_NODE, pairs))
    table = jnp.full((N_NODE, N_NODE, CAP), TOK_DEV, jnp.int32).at[home, source, slot].set(local_row)
    blocks = tok.reshape(N_NODE, TOK_DEV, D)
    padded = jnp.concatenate([blocks, jnp.zeros((N_NODE, 1, D), tok.dtype)], axis=1)
    gathered = padded[jnp.arange(N_NODE, dtype=jnp.int32)[None, :, None], table]
    group = FFE // N_LOCAL
    outputs = []
    for dest in range(N_NODE):
        rows = gathered[dest].reshape(N_NODE * CAP, D)
        total = jnp.zeros((N_NODE * CAP, D), jnp.float32)
        for part in range(N_LOCAL):
            lo = part * group
            gate = jnp.dot(rows, wg[dest][:, lo:lo + group], preferred_element_type=jnp.float32)
            upper = jnp.dot(rows, wu[dest][:, lo:lo + group], preferred_element_type=jnp.float32)
            hidden = (jax.nn.silu(gate) * upper).astype(jnp.bfloat16)
            piece = jnp.dot(hidden, wd[dest][lo:lo + group, :], preferred_element_type=jnp.float32).astype(jnp.bfloat16)
            total = total + piece.astype(jnp.float32)
        outputs.append(total.astype(jnp.bfloat16).reshape(N_NODE, CAP, D))
    expert_out = jnp.stack(outputs)
    picked = expert_out[home, source, slot].astype(jnp.float32)
    picked = picked.reshape(N_NODE, TOK_DEV, TOPK, D)
    weighted = jnp.sum(picked * gates.reshape(N_NODE, TOK_DEV, TOPK)[:, :, :, None], axis=2)
    result = blocks.astype(jnp.float32) + weighted
    return result.astype(jnp.bfloat16).reshape(TOKENS, D)


def reference(tokens, expert_ids, gate_weights, expert_node, w_gate, w_up, w_down):
    results = []
    for segment_index in range(N_SECTION):
        results.append(segment_layer(tokens[segment_index], expert_ids[segment_index], gate_weights[segment_index],
                                   expert_node[segment_index], w_gate[segment_index], w_up[segment_index], w_down[segment_index]))
    layer_out = jnp.stack(results)
    return jnp.roll(layer_out, 1, axis=0)
```

```python
import jax
import jax.numpy as jnp
from jax import lax
from jax.experimental import pallas as pl
from jax.experimental.pallas import tpu as pltpu
from jax.sharding import PartitionSpec as P

MESH = pl.DeviceIdType.MESH
BF = jnp.bfloat16
F32 = jnp.float32
RING = 4
CAP = 64
CHUNKS = 8
STAGES = 3
KEEP = 4


def kernel(ids_ref, gates_ref, place_ref, tok, wg_hbm, wu_hbm, wd_hbm, out,
           blocks, aux, pick, spread, staged, rows, rows_x, transit, acc_g, acc_u, wg, wu, wd, hid, hid_x,
           far, kept, far_in, near, near_in, done,
           w_sem, aux_s, aux_r, wd_s, wd_r, d_s, d_r, l_s, l_r, h_s, h_r, c_s, c_r, ready_q, ready_x):
    n_tok, feats = tok.shape
    width = feats // CHUNKS
    half = width // 2
    experts = place_ref.shape[1]
    core = lax.axis_index("local")
    section = lax.axis_index("section")
    node = lax.axis_index("node")
    z, y, x = node // 8, (node // 2) % 4, node % 2
    p = z + core * (y - z)
    q = y + core * (z - y)
    step_p = 8 - 6 * core
    step_q = 2 + 6 * core

    def at_node(dp, dq, dx):
        n = ((p + dp) % RING) * step_p + ((q + dq) % RING) * step_q + (x + dx) % 2
        return {"node": n, "local": core, "section": section}

    p_up, p_down = at_node(1, 0, 0), at_node(3, 0, 0)
    q_up, q_down = at_node(0, 1, 0), at_node(0, 3, 0)
    x_side = at_node(0, 0, 1)
    twin = {"node": node, "local": 1 - core, "section": section}
    after = {"node": node, "local": core, "section": 1 - section}

    def send(src, dst, s, r, to):
        return pltpu.make_async_remote_copy(src_ref=src, dst_ref=dst, send_sem=s, recv_sem=r,
                                            device_id=to, device_id_type=MESH)

    barrier = pltpu.get_barrier_semaphore()
    peers = (p_up, p_down, q_up, q_down, x_side, twin, after)
    for peer in peers:
        pl.semaphore_signal(barrier, inc=1, device_id=peer, device_id_type=MESH)
    pl.semaphore_wait(barrier, len(peers))

    def lanes(c):
        return pl.ds(pl.multiple_of(c * width, width), width)

    lo, hi = pl.ds(0, half), pl.ds(half, half)

    def d_p_up(c):
        return send(tok.at[:, lanes(c)], blocks.at[c, 0, 3], d_s.at[0, c], d_r.at[0, c], p_up)

    def d_p_down(c):
        return send(tok.at[:, lanes(c)], blocks.at[c, 0, 1], d_s.at[1, c], d_r.at[1, c], p_down)

    def d_f_up(c):
        return send(blocks.at[c, 0, 3, :, lo], blocks.at[c, 0, 2, :, lo], d_s.at[2, c], d_r.at[2, c], p_up)

    def d_f_down(c):
        return send(blocks.at[c, 0, 1, :, hi], blocks.at[c, 0, 2, :, hi], d_s.at[3, c], d_r.at[3, c], p_down)

    def d_x(c):
        return send(blocks.at[c, 0], blocks.at[c, 1], d_s.at[4, c], d_r.at[4, c], x_side)

    def d_q_up(c):
        return send(staged.at[c % STAGES, 0], rows.at[c, 3], d_s.at[5, c], d_r.at[5, c], q_up)

    def d_q_down(c):
        return send(staged.at[c % STAGES, 1], rows.at[c, 1], d_s.at[6, c], d_r.at[6, c], q_down)

    def d_t_up(c):
        return send(staged.at[c % STAGES, 2, :, :, :, lo], transit.at[c, 0], d_s.at[7, c], d_r.at[7, c], q_up)

    def d_t_down(c):
        return send(staged.at[c % STAGES, 2, :, :, :, hi], transit.at[c, 1], d_s.at[8, c], d_r.at[8, c], q_down)

    def d_u_up(c):
        return send(transit.at[c, 0], rows.at[c, 2, :, :, :, lo], d_s.at[9, c], d_r.at[9, c], q_up)

    def d_u_down(c):
        return send(transit.at[c, 1], rows.at[c, 2, :, :, :, hi], d_s.at[10, c], d_r.at[10, c], q_down)

    def d_twin(c, k):
        return send(rows.at[c, k], rows_x.at[c, :, k], l_s.at[k, c], l_r.at[k, c], twin)

    def h_twin(k):
        return send(hid.at[k], hid_x.at[:, k], h_s.at[k], h_r.at[k], twin)

    def c_q_up(c):
        return send(rows.at[c, 1], rows_x.at[c, 3], c_s.at[0, c], c_r.at[0, c], q_up)

    def c_q_down(c):
        return send(rows.at[c, 3], rows_x.at[c, 1], c_s.at[1, c], c_r.at[1, c], q_down)

    def c_t_up(c):
        return send(rows.at[c, 2, :, :, :, lo], rows_x.at[c, 0, :, :, :, lo], c_s.at[2, c], c_r.at[2, c], q_up)

    def c_t_down(c):
        return send(rows.at[c, 2, :, :, :, hi], rows_x.at[c, 0, :, :, :, hi], c_s.at[3, c], c_r.at[3, c], q_down)

    def c_u_up(c):
        return send(rows_x.at[c, 0, :, :, :, lo], rows_x.at[c, 2, :, :, :, lo], c_s.at[4, c], c_r.at[4, c], q_up)

    def c_u_down(c):
        return send(rows_x.at[c, 0, :, :, :, hi], rows_x.at[c, 2, :, :, :, hi], c_s.at[5, c], c_r.at[5, c], q_down)

    def c_x(c):
        return send(blocks.at[c, 0], blocks.at[c, 1], c_s.at[6, c], c_r.at[6, c], x_side)

    def c_f_up(c):
        return send(far.at[c, :, lo], far_in.at[c, 0], c_s.at[7, c], c_r.at[7, c], p_up)

    def c_f_down(c):
        return send(far.at[c, :, hi], far_in.at[c, 1], c_s.at[8, c], c_r.at[8, c], p_down)

    def c_p_up(c):
        return send(near.at[c, 0], near_in.at[c, 0], c_s.at[9, c], c_r.at[9, c], p_up)

    def c_p_down(c):
        return send(near.at[c, 1], near_in.at[c, 1], c_s.at[10, c], c_r.at[10, c], p_down)

    def c_out(c):
        return send(done.at[c], out.at[:, lanes(c)], c_s.at[11, c], c_r.at[11, c], after)

    load_g = pltpu.make_async_copy(wg_hbm.at[0, 0], wg, w_sem.at[0])
    load_u = pltpu.make_async_copy(wu_hbm.at[0, 0], wu, w_sem.at[1])
    load_d = pltpu.make_async_copy(
        wd_hbm.at[0, 0, :, pl.ds(pl.multiple_of(core * feats, feats), feats)], wd.at[0], w_sem.at[2])
    give_d = send(wd_hbm.at[0, 0, :, pl.ds(pl.multiple_of((1 - core) * feats, feats), feats)], wd.at[1],
                  wd_s.at[0], wd_r.at[0], twin)

    ids = ids_ref[...]
    home = jnp.zeros_like(ids)
    for e in range(experts):
        home = jnp.where(ids == e, place_ref[0, e], home)
    m_index = lax.broadcasted_iota(jnp.int32, (experts, n_tok), 0)
    chosen = jnp.zeros((experts, n_tok), F32)
    weight = jnp.zeros((experts, n_tok), F32)
    for k in range(ids.shape[0]):
        same = home[k:k + 1, :] == m_index
        chosen = chosen + jnp.where(same, 1.0, 0.0)
        weight = weight + jnp.where(same, gates_ref[k:k + 1, :], 0.0)
    earlier = jnp.where(lax.broadcasted_iota(jnp.int32, (n_tok, n_tok), 0)
                        < lax.broadcasted_iota(jnp.int32, (n_tok, n_tok), 1), 1.0, 0.0).astype(BF)
    count = jnp.dot(chosen.astype(BF), earlier, preferred_element_type=F32)
    aux[0, 0, :experts, :] = jnp.where(chosen > 0.5, count, -1.0)
    aux[0, 0, experts:, :] = weight

    a_up = send(aux.at[0, 0], aux.at[0, 3], aux_s.at[0], aux_r.at[0], p_up)
    a_down = send(aux.at[0, 0], aux.at[0, 1], aux_s.at[1], aux_r.at[1], p_down)
    a_f = send(aux.at[0, 3], aux.at[0, 2], aux_s.at[2], aux_r.at[2], p_up)
    a_x = send(aux.at[0], aux.at[1], aux_s.at[3], aux_r.at[3], x_side)
    a_up.start()
    a_down.start()
    AHEAD = 3
    for c in range(AHEAD):
        d_p_up(c).start()
        d_p_down(c).start()
    load_g.start()
    load_u.start()
    load_d.start()
    give_d.start()

    @pl.loop(0, CHUNKS)
    def _(c):
        blocks[c, 0, 0] = tok[:, lanes(c)]

    acc_g[...] = jnp.zeros_like(acc_g)
    acc_u[...] = jnp.zeros_like(acc_u)
    a_up.wait_recv()
    a_down.wait_recv()
    a_f.start()
    a_f.wait_recv()
    a_x.start()
    slot_index = lax.broadcasted_iota(jnp.int32, (CAP, n_tok), 0).astype(F32)

    def tables(side):
        @pl.loop(0, RING)
        def _(b):
            parts = []
            for k in range(RING):
                m = p * step_p + ((q + k) % RING) * step_q + x
                here = aux[side, b, pl.ds(m, 1), :] == slot_index
                pick[side, b, k * CAP:(k + 1) * CAP, :] = jnp.where(here, 1.0, 0.0).astype(BF)
                parts.append(jnp.where(here, aux[side, b, pl.ds(experts + m, 1), :], 0.0))
            whole = jnp.concatenate(parts, axis=0).T
            top = whole.astype(BF)
            spread[0, side, b] = top
            spread[1, side, b] = (whole - top.astype(F32)).astype(BF)

    tables(0)
    a_x.wait_recv()
    tables(1)
    load_g.wait()
    load_u.wait()

    def accumulate(c):
        own = pl.ds(pl.multiple_of(core * feats + c * width, width), width)
        other = pl.ds(pl.multiple_of((1 - core) * feats + c * width, width), width)

        @pl.loop(0, 2 * RING)
        def _(t):
            k, b = t // 2, (t % 2) * 2
            mine = rows[c, k, pl.ds(b, 2)].reshape(4 * CAP, width)
            theirs = rows_x[c, k, pl.ds(b, 2)].reshape(4 * CAP, width)
            where = pl.ds(pl.multiple_of(t * 4 * CAP, 4 * CAP), 4 * CAP)
            acc_g[where, :] += (jnp.dot(mine, wg[own, :], preferred_element_type=F32)
                                + jnp.dot(theirs, wg[other, :], preferred_element_type=F32))
            acc_u[where, :] += (jnp.dot(mine, wu[own, :], preferred_element_type=F32)
                                + jnp.dot(theirs, wu[other, :], preferred_element_type=F32))

    def within(c):
        return (c >= 0) & (c < CHUNKS)

    @pl.loop(0, CHUNKS + 6)
    def _(i):
        @pl.when(i + AHEAD < CHUNKS)
        def _():
            d_p_up(i + AHEAD).start()
            d_p_down(i + AHEAD).start()

        @pl.when(within(i))
        def _():
            d_p_up(i).wait_recv()
            d_f_up(i).start()
            d_p_down(i).wait_recv()
            d_f_down(i).start()

        @pl.when(within(i - 1))
        def _():
            c = i - 1
            d_f_up(c).wait_recv()
            d_f_down(c).wait_recv()
            d_x(c).start()

        @pl.when(within(i - 2))
        def _():
            c = i - 2

            @pl.when(c >= STAGES)
            def _():
                d_q_up(c - STAGES).wait_send()
                d_q_down(c - STAGES).wait_send()
                d_t_up(c - STAGES).wait_send()
                d_t_down(c - STAGES).wait_send()

            d_x(c).wait_recv()
            for side in range(2):
                for b in range(RING):
                    got = jnp.dot(pick[side, b], blocks[c, side, b], preferred_element_type=F32).astype(BF)
                    rows[c, 0, b, side] = got[:CAP]
                    staged[c % STAGES, 0, b, side] = got[CAP:2 * CAP]
                    staged[c % STAGES, 2, b, side] = got[2 * CAP:3 * CAP]
                    staged[c % STAGES, 1, b, side] = got[3 * CAP:]
            d_t_up(c).start()
            d_t_down(c).start()
            d_q_up(c).start()
            d_q_down(c).start()
            d_twin(c, 0).start()

        @pl.when(within(i - 3))
        def _():
            c = i - 3
            d_t_up(c).wait_recv()
            d_u_up(c).start()
            d_t_down(c).wait_recv()
            d_u_down(c).start()

        @pl.when(within(i - 4))
        def _():
            c = i - 4
            d_q_up(c).wait_recv()
            d_twin(c, 3).start()
            d_q_down(c).wait_recv()
            d_twin(c, 1).start()
            d_u_up(c).wait_recv()
            d_u_down(c).wait_recv()
            d_twin(c, 2).start()

        @pl.when(within(i - 5))
        def _():
            c = i - 5
            for k in range(RING):
                d_twin(c, k).wait_recv()
            accumulate(c)

    pl.semaphore_signal(ready_q, inc=1, device_id=q_up, device_id_type=MESH)
    pl.semaphore_signal(ready_q, inc=1, device_id=q_down, device_id_type=MESH)
    pl.semaphore_signal(ready_x, inc=1, device_id=x_side, device_id_type=MESH)

    for k in range(RING):
        @pl.loop(0, 2)
        def _(t):
            where = pl.ds(pl.multiple_of((2 * k + t) * 4 * CAP, 4 * CAP), 4 * CAP)
            g = acc_g[where, :]
            h = g / (1.0 + jnp.exp(-g)) * acc_u[where, :]
            hid[k, pl.ds(t * 2, 2)] = h.astype(BF).reshape(2, 2, CAP, h.shape[-1])
        h_twin(k).start()

    @pl.loop(0, CHUNKS)
    def _(c):
        for copy in (d_p_up, d_p_down, d_f_up, d_f_down, d_x, d_u_up, d_u_down):
            copy(c).wait_send()
        for k in range(RING):
            d_twin(c, k).wait_send()

    @pl.loop(CHUNKS - STAGES, CHUNKS)
    def _(c):
        for copy in (d_q_up, d_q_down, d_t_up, d_t_down):
            copy(c).wait_send()
    for copy in (a_up, a_down, a_f, a_x):
        copy.wait_send()
    load_d.wait()
    give_d.wait()
    for k in range(RING):
        h_twin(k).wait_recv()
    pl.semaphore_wait(ready_q, 2)
    pl.semaphore_wait(ready_x, 1)

    def spread_out(c, side, b):
        got = jnp.concatenate(
            [rows[c, 0, b, side], rows_x[c, 1, b, side], rows_x[c, 2, b, side], rows_x[c, 3, b, side]], axis=0)
        return (jnp.dot(spread[0, side, b], got, preferred_element_type=F32)
                + jnp.dot(spread[1, side, b], got, preferred_element_type=F32))

    @pl.loop(0, CHUNKS + 5)
    def _(i):
        @pl.when(within(i))
        def _():
            c = i

            @pl.loop(0, 2 * RING)
            def _(t):
                k, b = t // 2, (t % 2) * 2
                mine = hid[k, pl.ds(b, 2)].reshape(4 * CAP, hid.shape[-1])
                theirs = hid_x[k, pl.ds(b, 2)].reshape(4 * CAP, hid.shape[-1])
                made = (jnp.dot(mine, wd[0, :, lanes(c)], preferred_element_type=F32)
                        + jnp.dot(theirs, wd[1, :, lanes(c)], preferred_element_type=F32))
                rows[c, k, pl.ds(b, 2)] = made.astype(BF).reshape(2, 2, CAP, width)

            c_t_up(c).start()
            c_t_down(c).start()
            c_q_up(c).start()
            c_q_down(c).start()

        @pl.when(within(i - 1))
        def _():
            c = i - 1
            c_t_up(c).wait_recv()
            c_u_up(c).start()
            c_t_down(c).wait_recv()
            c_u_down(c).start()

        @pl.when(within(i - 2))
        def _():
            c = i - 2
            c_q_up(c).wait_recv()
            c_q_down(c).wait_recv()
            c_u_up(c).wait_recv()
            c_u_down(c).wait_recv()
            for b in range(RING):
                blocks[c, 0, b] = spread_out(c, 1, b).astype(BF)
            c_x(c).start()

        @pl.when(within(i - 3))
        def _():
            c = i - 3
            c_x(c).wait_recv()
            far[c] = (spread_out(c, 0, 2) + blocks[c, 1, 2].astype(F32)).astype(BF)
            c_f_up(c).start()
            c_f_down(c).start()
            for place, b in enumerate((0, 1, 3)):
                kept[c % KEEP, place] = spread_out(c, 0, b) + blocks[c, 1, b].astype(F32)

        @pl.when(within(i - 4))
        def _():
            c = i - 4
            c_f_up(c).wait_recv()
            near[c, 0, :, :half] = (kept[c % KEEP, 1, :, :half] + far_in[c, 0].astype(F32)).astype(BF)
            near[c, 0, :, half:] = kept[c % KEEP, 1, :, half:].astype(BF)
            c_p_up(c).start()
            c_f_down(c).wait_recv()
            near[c, 1, :, :half] = kept[c % KEEP, 2, :, :half].astype(BF)
            near[c, 1, :, half:] = (kept[c % KEEP, 2, :, half:] + far_in[c, 1].astype(F32)).astype(BF)
            c_p_down(c).start()

        @pl.when(within(i - 5))
        def _():
            c = i - 5
            c_p_up(c).wait_recv()
            c_p_down(c).wait_recv()
            total = kept[c % KEEP, 0] + near_in[c, 0].astype(F32) + near_in[c, 1].astype(F32)
            done[c] = (total + tok[:, lanes(c)].astype(F32)).astype(BF)
            c_out(c).start()

    for k in range(RING):
        h_twin(k).wait_send()

    @pl.loop(0, CHUNKS)
    def _(c):
        c_out(c).wait_recv()
        for copy in (c_q_up, c_q_down, c_t_up, c_t_down, c_u_up, c_u_down, c_x, c_f_up, c_f_down,
                     c_p_up, c_p_down, c_out):
            copy(c).wait_send()


def body(tokens, expert_ids, gate_weights, expert_node, w_gate, w_up, w_down):
    own = tokens[0]
    n_tok, feats = own.shape
    width = feats // CHUNKS
    hidden = w_gate.shape[3]
    deep = w_gate.shape[2]
    total = 8 * RING * CAP
    vmem = pl.BlockSpec(memory_space=pltpu.VMEM)
    anywhere = pl.BlockSpec(memory_space=pl.ANY)
    dma = pltpu.SemaphoreType.DMA
    held = pltpu.VMEM
    out = pl.pallas_call(
        kernel,
        out_shape=jax.ShapeDtypeStruct((n_tok, feats), BF),
        in_specs=[vmem, vmem, pl.BlockSpec(memory_space=pltpu.SMEM), vmem, anywhere, anywhere, anywhere],
        out_specs=anywhere,
        scratch_shapes=[
            held((CHUNKS, 2, RING, n_tok, width), BF),
            held((2, RING, 2 * expert_node.shape[1], n_tok), F32),
            held((2, RING, RING * CAP, n_tok), BF),
            held((2, 2, RING, n_tok, RING * CAP), BF),
            held((STAGES, 3, RING, 2, CAP, width), BF),
            held((CHUNKS, RING, RING, 2, CAP, width), BF),
            held((CHUNKS, RING, RING, 2, CAP, width), BF),
            held((CHUNKS, 2, RING, 2, CAP, width // 2), BF),
            held((total, hidden), F32),
            held((total, hidden), F32),
            held((deep, hidden), BF),
            held((deep, hidden), BF),
            held((2, hidden, feats), BF),
            held((RING, RING, 2, CAP, hidden), BF),
            held((RING, RING, 2, CAP, hidden), BF),
            held((CHUNKS, n_tok, width), BF),
            held((KEEP, 3, n_tok, width), F32),
            held((CHUNKS, 2, n_tok, width // 2), BF),
            held((CHUNKS, 2, n_tok, width), BF),
            held((CHUNKS, 2, n_tok, width), BF),
            held((CHUNKS, n_tok, width), BF),
            dma((3,)),
            dma((4,)),
            dma((4,)),
            dma((1,)),
            dma((1,)),
            dma((11, CHUNKS)),
            dma((11, CHUNKS)),
            dma((RING, CHUNKS)),
            dma((RING, CHUNKS)),
            dma((RING,)),
            dma((RING,)),
            dma((12, CHUNKS)),
            dma((12, CHUNKS)),
            pltpu.SemaphoreType.REGULAR,
            pltpu.SemaphoreType.REGULAR,
        ],
        compiler_params=pltpu.CompilerParams(
            collective_id=0, has_side_effects=True, vmem_limit_bytes=60 * 1024 * 1024),
        name="expert_layer",
    )(expert_ids[0].T, gate_weights[0].T, expert_node, own, w_gate, w_up, w_down)
    return out[None]


def solution(mesh):
    in_specs = (
        P("section", "node", "local"),
        P("section", "node", None),
        P("section", "node", None),
        P("section", None),
        P("section", "node", None, "local"),
        P("section", "node", None, "local"),
        P("section", "node", "local", None),
    )
    out_specs = P("section", "node", "local")
    return jax.shard_map(body, mesh=mesh, in_specs=in_specs, out_specs=out_specs, check_vma=False)
```

```python
import jax
import jax.numpy as jnp
from jax import lax
from jax.experimental import pallas as pl
from jax.experimental.pallas import tpu as pltpu
from jax.sharding import PartitionSpec as P

MESH = pl.DeviceIdType.MESH
BF = jnp.bfloat16
F32 = jnp.float32
RING = 4
CAP = 64
CHUNKS = 8
STAGES = 3
LAG = 2
X_AHEAD = 2


def kernel(ids_ref, gates_ref, place_ref, tok, wg_hbm, wu_hbm, wd_hbm, out,
           blocks, aux, pick, spread, first, staged, staged_x, rows, rows_x, acc_g, acc_u, wg, wu, wd, hid, hid_x,
           pair_in, parts,
           w_sem, aux_s, aux_r, wd_s, wd_r, o_s, o_r, d_s, d_r, l_s, l_r, h_s, h_r, c_s, c_r, ready_q):
    n_tok, feats = tok.shape
    width = feats // CHUNKS
    experts = place_ref.shape[1]
    core = lax.axis_index("local")
    section = lax.axis_index("section")
    node = lax.axis_index("node")
    z, y, x = node // 8, (node // 2) % 4, node % 2
    p = z + core * (y - z)
    q = y + core * (z - y)
    step_p = 8 - 6 * core
    step_q = 2 + 6 * core

    def at_node(dp, dq, dx, segment=section):
        n = ((p + dp) % RING) * step_p + ((q + dq) % RING) * step_q + (x + dx) % 2
        return {"node": n, "local": core, "section": segment}

    p_peer = [None] + [at_node(d, 0, 0) for d in range(1, RING)]
    q_peer = [None] + [at_node(0, d, 0) for d in range(1, RING)]
    x_side = at_node(0, 0, 1)
    twin = {"node": node, "local": 1 - core, "section": section}
    over = [at_node(d, 0, 1, 1 - section) for d in range(RING)]

    def send(src, dst, s, r, to):
        return pltpu.make_async_remote_copy(src_ref=src, dst_ref=dst, send_sem=s, recv_sem=r,
                                            device_id=to, device_id_type=MESH)

    barrier = pltpu.get_barrier_semaphore()
    peers = p_peer[1:] + q_peer[1:] + [x_side, twin] + over
    for peer in peers:
        pl.semaphore_signal(barrier, inc=1, device_id=peer, device_id_type=MESH)
    pl.semaphore_wait(barrier, len(peers))

    def lanes(c):
        return pl.ds(pl.multiple_of(c * width, width), width)

    def d_p(c, d):
        return send(tok.at[:, lanes(c)], blocks.at[c, 0, RING - d], d_s.at[d, c], d_r.at[d, c], p_peer[d])

    def d_x_own(c):
        return send(blocks.at[c, 0, 0], blocks.at[c, 1, 0], d_s.at[0, c], d_r.at[0, c], x_side)

    def d_x(c):
        return send(blocks.at[c, 0, pl.ds(1, 3)], blocks.at[c, 1, pl.ds(1, 3)], d_s.at[4, c], d_r.at[4, c], x_side)

    def d_first(d):
        return send(first.at[d - 1], rows.at[:, RING - d, 0, 0], o_s.at[d - 1], o_r.at[d - 1], q_peer[d])

    def d_q(c, d):
        return send(staged.at[c % STAGES, d - 1], rows.at[c, RING - d, pl.ds(1, 3), 0],
                    d_s.at[4 + d, c], d_r.at[4 + d, c], q_peer[d])

    def d_qx(c, d):
        return send(staged_x.at[c % STAGES, d - 1], rows.at[c, RING - d, :, 1],
                    d_s.at[7 + d, c], d_r.at[7 + d, c], q_peer[d])

    def d_twin(c, k):
        return send(rows.at[c, k], rows_x.at[c, :, k], l_s.at[k, c], l_r.at[k, c], twin)

    def h_twin(k):
        return send(hid.at[k], hid_x.at[:, k], h_s.at[k], h_r.at[k], twin)

    def c_q(c, d):
        return send(rows.at[c, d], rows_x.at[c, RING - d], c_s.at[d, c], c_r.at[d, c], q_peer[d])

    def c_x(c):
        return send(blocks.at[c, 0], pair_in.at[c], c_s.at[0, c], c_r.at[0, c], x_side)

    def c_over(c, d):
        return send(blocks.at[c, 1, d], parts.at[c, d], c_s.at[4 + d, c], c_r.at[4 + d, c], over[d])

    load_g = pltpu.make_async_copy(wg_hbm.at[0, 0], wg, w_sem.at[0])
    load_u = pltpu.make_async_copy(wu_hbm.at[0, 0], wu, w_sem.at[1])
    load_d = pltpu.make_async_copy(
        wd_hbm.at[0, 0, :, pl.ds(pl.multiple_of(core * feats, feats), feats)], wd.at[0], w_sem.at[2])
    give_d = send(wd_hbm.at[0, 0, :, pl.ds(pl.multiple_of((1 - core) * feats, feats), feats)], wd.at[1],
                  wd_s.at[0], wd_r.at[0], twin)

    for c in range(CHUNKS):
        for d in (1, 3, 2):
            d_p(c, d).start()

    ids = ids_ref[...]
    home = jnp.zeros_like(ids)
    for e in range(experts):
        home = jnp.where(ids == e, place_ref[0, e], home)
    m_index = lax.broadcasted_iota(jnp.int32, (experts, n_tok), 0)
    chosen = jnp.zeros((experts, n_tok), F32)
    weight = jnp.zeros((experts, n_tok), F32)
    for k in range(ids.shape[0]):
        same = home[k:k + 1, :] == m_index
        chosen = chosen + jnp.where(same, 1.0, 0.0)
        weight = weight + jnp.where(same, gates_ref[k:k + 1, :], 0.0)
    earlier = jnp.where(lax.broadcasted_iota(jnp.int32, (n_tok, n_tok), 0)
                        < lax.broadcasted_iota(jnp.int32, (n_tok, n_tok), 1), 1.0, 0.0).astype(BF)
    count = jnp.dot(chosen.astype(BF), earlier, preferred_element_type=F32)
    aux[0, 0, :experts, :] = jnp.where(chosen > 0.5, count, -1.0)
    aux[0, 0, experts:, :] = weight

    a_p = [None] + [send(aux.at[0, 0], aux.at[0, RING - d], aux_s.at[d], aux_r.at[d], p_peer[d])
                    for d in range(1, RING)]
    a_x = send(aux.at[0], aux.at[1], aux_s.at[0], aux_r.at[0], x_side)
    for d in range(1, RING):
        a_p[d].start()

    slot_index = lax.broadcasted_iota(jnp.int32, (CAP, n_tok), 0).astype(F32)

    def table(side, b):
        parts_of = []
        for k in range(RING):
            m = p * step_p + ((q + k) % RING) * step_q + x
            here = aux[side, b, pl.ds(m, 1), :] == slot_index
            pick[side, b, k * CAP:(k + 1) * CAP, :] = jnp.where(here, 1.0, 0.0).astype(BF)
            parts_of.append(jnp.where(here, aux[side, b, pl.ds(experts + m, 1), :], 0.0))
        whole = jnp.concatenate(parts_of, axis=0).T
        top = whole.astype(BF)
        spread[0, side, b] = top
        spread[1, side, b] = (whole - top.astype(F32)).astype(BF)

    table(0, 0)
    for c in range(CHUNKS):
        mine = tok[:, c * width:(c + 1) * width]
        blocks[c, 0, 0] = mine
        if c < X_AHEAD:
            d_x_own(c).start()
        got = jnp.dot(pick[0, 0], mine, preferred_element_type=F32).astype(BF)
        rows[c, 0, 0, 0] = got[:CAP]
        for d in range(1, RING):
            first[d - 1, c] = got[d * CAP:(d + 1) * CAP]
    for d in (2, 1, 3):
        d_first(d).start()
    load_g.start()
    load_u.start()
    load_d.start()
    give_d.start()
    for d in range(1, RING):
        a_p[d].wait_recv()
    a_x.start()

    @pl.loop(1, RING)
    def _(b):
        table(0, b)

    acc_g[...] = jnp.zeros_like(acc_g)
    acc_u[...] = jnp.zeros_like(acc_u)

    def accumulate(c):
        own = pl.ds(pl.multiple_of(core * feats + c * width, width), width)
        other = pl.ds(pl.multiple_of((1 - core) * feats + c * width, width), width)

        @pl.loop(0, 2 * RING)
        def _(t):
            k, b = t // 2, (t % 2) * 2
            mine = rows[c, k, pl.ds(b, 2)].reshape(4 * CAP, width)
            theirs = rows_x[c, k, pl.ds(b, 2)].reshape(4 * CAP, width)
            where = pl.ds(pl.multiple_of(t * 4 * CAP, 4 * CAP), 4 * CAP)
            acc_g[where, :] += (jnp.dot(mine, wg[own, :], preferred_element_type=F32)
                                + jnp.dot(theirs, wg[other, :], preferred_element_type=F32))
            acc_u[where, :] += (jnp.dot(mine, wu[own, :], preferred_element_type=F32)
                                + jnp.dot(theirs, wu[other, :], preferred_element_type=F32))

    def within(c):
        return (c >= 0) & (c < CHUNKS)

    @pl.loop(0, CHUNKS + LAG + 2)
    def _(i):
        @pl.when(within(i))
        def _():
            c = i
            for d in (1, 3, 2):
                d_p(c, d).wait_recv()
            d_x(c).start()

            @pl.when(c + X_AHEAD < CHUNKS)
            def _():
                d_x_own(c + X_AHEAD).start()

            @pl.when(c >= STAGES)
            def _():
                for d in range(1, RING):
                    d_q(c - STAGES, d).wait_send()

            for b in range(1, RING):
                got = jnp.dot(pick[0, b], blocks[c, 0, b], preferred_element_type=F32).astype(BF)
                rows[c, 0, b, 0] = got[:CAP]
                for d in range(1, RING):
                    staged[c % STAGES, d - 1, b - 1] = got[d * CAP:(d + 1) * CAP]
            for d in (2, 1, 3):
                d_q(c, d).start()

        @pl.when(i == LAG - 1)
        def _():
            a_x.wait_recv()

            @pl.loop(0, RING)
            def _(b):
                table(1, b)

        @pl.when(within(i - LAG))
        def _():
            c = i - LAG
            d_x_own(c).wait_recv()
            d_x(c).wait_recv()

            @pl.when(c >= STAGES)
            def _():
                for d in range(1, RING):
                    d_qx(c - STAGES, d).wait_send()

            for b in range(RING):
                got = jnp.dot(pick[1, b], blocks[c, 1, b], preferred_element_type=F32).astype(BF)
                rows[c, 0, b, 1] = got[:CAP]
                for d in range(1, RING):
                    staged_x[c % STAGES, d - 1, b] = got[d * CAP:(d + 1) * CAP]
            for d in (2, 1, 3):
                d_qx(c, d).start()
            d_twin(c, 0).start()

        @pl.when(within(i - LAG - 1))
        def _():
            c = i - LAG - 1

            @pl.when(c == 0)
            def _():
                for d in range(1, RING):
                    d_first(d).wait_recv()
            for d in range(1, RING):
                d_q(c, d).wait_recv()
                d_qx(c, d).wait_recv()
                d_twin(c, RING - d).start()

        @pl.when(within(i - LAG - 2))
        def _():
            c = i - LAG - 2

            @pl.when(c == 0)
            def _():
                load_g.wait()
                load_u.wait()
            for k in range(RING):
                d_twin(c, k).wait_recv()
            accumulate(c)

    for d in range(1, RING):
        pl.semaphore_signal(ready_q, inc=1, device_id=q_peer[d], device_id_type=MESH)

    for k in range(RING):
        @pl.loop(0, 2)
        def _(t):
            where = pl.ds(pl.multiple_of((2 * k + t) * 4 * CAP, 4 * CAP), 4 * CAP)
            g = acc_g[where, :]
            h = g / (1.0 + jnp.exp(-g)) * acc_u[where, :]
            hid[k, pl.ds(t * 2, 2)] = h.astype(BF).reshape(2, 2, CAP, h.shape[-1])
        h_twin(k).start()

    @pl.loop(0, CHUNKS)
    def _(c):
        for d in range(1, RING):
            d_p(c, d).wait_send()
        d_x_own(c).wait_send()
        d_x(c).wait_send()
        for k in range(RING):
            d_twin(c, k).wait_send()

    @pl.loop(CHUNKS - STAGES, CHUNKS)
    def _(c):
        for d in range(1, RING):
            d_q(c, d).wait_send()
            d_qx(c, d).wait_send()
    for d in range(1, RING):
        a_p[d].wait_send()
        d_first(d).wait_send()
    a_x.wait_send()
    load_d.wait()
    give_d.wait()
    for k in range(RING):
        h_twin(k).wait_recv()
    pl.semaphore_wait(ready_q, RING - 1)

    def spread_out(c, side, b):
        got = jnp.concatenate(
            [rows[c, 0, b, side], rows_x[c, 1, b, side], rows_x[c, 2, b, side], rows_x[c, 3, b, side]], axis=0)
        return (jnp.dot(spread[0, side, b], got, preferred_element_type=F32)
                + jnp.dot(spread[1, side, b], got, preferred_element_type=F32))

    @pl.loop(0, CHUNKS + 3)
    def _(i):
        @pl.when(within(i))
        def _():
            c = i

            @pl.loop(0, 2 * RING)
            def _(t):
                k, b = t // 2, (t % 2) * 2
                mine = hid[k, pl.ds(b, 2)].reshape(4 * CAP, hid.shape[-1])
                theirs = hid_x[k, pl.ds(b, 2)].reshape(4 * CAP, hid.shape[-1])
                made = (jnp.dot(mine, wd[0, :, lanes(c)], preferred_element_type=F32)
                        + jnp.dot(theirs, wd[1, :, lanes(c)], preferred_element_type=F32))
                rows[c, k, pl.ds(b, 2)] = made.astype(BF).reshape(2, 2, CAP, width)

            for d in (2, 1, 3):
                c_q(c, d).start()

        @pl.when(within(i - 1))
        def _():
            c = i - 1
            for d in range(1, RING):
                c_q(c, d).wait_recv()
            for b in range(RING):
                blocks[c, 0, b] = spread_out(c, 0, b).astype(BF)
            c_x(c).start()

        @pl.when(within(i - 2))
        def _():
            c = i - 2
            c_x(c).wait_recv()
            for b in (2, 1, 3, 0):
                total = spread_out(c, 1, b) + pair_in[c, b].astype(F32)
                if b == 0:
                    total = total + blocks[c, 1, 0].astype(F32)
                blocks[c, 1, b] = total.astype(BF)
                c_over(c, b).start()

        @pl.when(within(i - 3))
        def _():
            c = i - 3
            for d in range(RING):
                c_over(c, d).wait_recv()
            total = parts[c, 0].astype(F32) + parts[c, 1].astype(F32)
            total = total + parts[c, 2].astype(F32) + parts[c, 3].astype(F32)
            out[:, lanes(c)] = total.astype(BF)

    for k in range(RING):
        h_twin(k).wait_send()

    @pl.loop(0, CHUNKS)
    def _(c):
        for d in range(1, RING):
            c_q(c, d).wait_send()
        c_x(c).wait_send()
        for d in range(RING):
            c_over(c, d).wait_send()


def body(tokens, expert_ids, gate_weights, expert_node, w_gate, w_up, w_down):
    own = tokens[0]
    n_tok, feats = own.shape
    width = feats // CHUNKS
    hidden = w_gate.shape[3]
    deep = w_gate.shape[2]
    total = 8 * RING * CAP
    vmem = pl.BlockSpec(memory_space=pltpu.VMEM)
    anywhere = pl.BlockSpec(memory_space=pl.ANY)
    dma = pltpu.SemaphoreType.DMA
    held = pltpu.VMEM
    out = pl.pallas_call(
        kernel,
        out_shape=jax.ShapeDtypeStruct((n_tok, feats), BF),
        in_specs=[vmem, vmem, pl.BlockSpec(memory_space=pltpu.SMEM), vmem, anywhere, anywhere, anywhere],
        out_specs=vmem,
        scratch_shapes=[
            held((CHUNKS, 2, RING, n_tok, width), BF),
            held((2, RING, 2 * expert_node.shape[1], n_tok), F32),
            held((2, RING, RING * CAP, n_tok), BF),
            held((2, 2, RING, n_tok, RING * CAP), BF),
            held((RING - 1, CHUNKS, CAP, width), BF),
            held((STAGES, RING - 1, RING - 1, CAP, width), BF),
            held((STAGES, RING - 1, RING, CAP, width), BF),
            held((CHUNKS, RING, RING, 2, CAP, width), BF),
            held((CHUNKS, RING, RING, 2, CAP, width), BF),
            held((total, hidden), F32),
            held((total, hidden), F32),
            held((deep, hidden), BF),
            held((deep, hidden), BF),
            held((2, hidden, feats), BF),
            held((RING, RING, 2, CAP, hidden), BF),
            held((RING, RING, 2, CAP, hidden), BF),
            held((CHUNKS, RING, n_tok, width), BF),
            held((CHUNKS, RING, n_tok, width), BF),
            dma((3,)),
            dma((RING,)),
            dma((RING,)),
            dma((1,)),
            dma((1,)),
            dma((RING - 1,)),
            dma((RING - 1,)),
            dma((11, CHUNKS)),
            dma((11, CHUNKS)),
            dma((RING, CHUNKS)),
            dma((RING, CHUNKS)),
            dma((RING,)),
            dma((RING,)),
            dma((8, CHUNKS)),
            dma((8, CHUNKS)),
            pltpu.SemaphoreType.REGULAR,
        ],
        compiler_params=pltpu.CompilerParams(
            collective_id=0, has_side_effects=True, vmem_limit_bytes=60 * 1024 * 1024),
        name="expert_layer",
    )(expert_ids[0].T, gate_weights[0].T, expert_node, own, w_gate, w_up, w_down)
    return out[None]


def solution(mesh):
    in_specs = (
        P("section", "node", "local"),
        P("section", "node", None),
        P("section", "node", None),
        P("section", None),
        P("section", "node", None, "local"),
        P("section", "node", None, "local"),
        P("section", "node", "local", None),
    )
    out_specs = P("section", "node", "local")
    return jax.shard_map(body, mesh=mesh, in_specs=in_specs, out_specs=out_specs, check_vma=False)
```

```python
import jax
import jax.numpy as jnp
from jax import lax
from jax.experimental import pallas as pl
from jax.experimental.pallas import tpu as pltpu
from jax.sharding import PartitionSpec as P

MESH = pl.DeviceIdType.MESH
BF = jnp.bfloat16
F32 = jnp.float32
RING = 4
CAP = 64
CHUNKS = 8
STAGES = 3
LAG = 2
SHARE = 1
ADD = 2
P_AHEAD = 2
X_AHEAD = 2


def kernel(ids_ref, gates_ref, place_ref, tok, wg_hbm, wu_hbm, wd_hbm, out,
           blocks, aux, pick, spread, first, staged, staged_x, rows, rows_x, acc_g, acc_u, wg, wu, wd, hid, hid_x,
           pair_in, parts,
           w_sem, aux_s, aux_r, wd_s, wd_r, o_s, o_r, d_s, d_r, l_s, l_r, h_s, h_r, c_s, c_r, x_s, x_r, ready_q):
    n_tok, feats = tok.shape
    width = feats // CHUNKS
    experts = place_ref.shape[1]
    core = lax.axis_index("local")
    section = lax.axis_index("section")
    node = lax.axis_index("node")
    z, y, x = node // 8, (node // 2) % 4, node % 2
    p = z + core * (y - z)
    q = y + core * (z - y)
    step_p = 8 - 6 * core
    step_q = 2 + 6 * core

    def at_node(dp, dq, dx, segment=section):
        n = ((p + dp) % RING) * step_p + ((q + dq) % RING) * step_q + (x + dx) % 2
        return {"node": n, "local": core, "section": segment}

    p_peer = [None] + [at_node(d, 0, 0) for d in range(1, RING)]
    q_peer = [None] + [at_node(0, d, 0) for d in range(1, RING)]
    x_side = at_node(0, 0, 1)
    twin = {"node": node, "local": 1 - core, "section": section}
    over = [at_node(d, 0, 1, 1 - section) for d in range(RING)]

    def send(src, dst, s, r, to):
        return pltpu.make_async_remote_copy(src_ref=src, dst_ref=dst, send_sem=s, recv_sem=r,
                                            device_id=to, device_id_type=MESH)

    barrier = pltpu.get_barrier_semaphore()
    peers = p_peer[1:] + q_peer[1:] + [x_side, twin] + over
    for peer in peers:
        pl.semaphore_signal(barrier, inc=1, device_id=peer, device_id_type=MESH)
    pl.semaphore_wait(barrier, len(peers))

    def lanes(c):
        return pl.ds(pl.multiple_of(c * width, width), width)

    def d_p(c, d):
        return send(tok.at[:, lanes(c)], blocks.at[c, 0, RING - d], d_s.at[d, c], d_r.at[d, c], p_peer[d])

    def d_x_own(c):
        return send(blocks.at[c, 0, 0], blocks.at[c, 1, 0], d_s.at[0, c], d_r.at[0, c], x_side)

    def d_x(c):
        return send(blocks.at[c, 0, pl.ds(1, 3)], blocks.at[c, 1, pl.ds(1, 3)], d_s.at[4, c], d_r.at[4, c], x_side)

    def d_first(d):
        return send(first.at[d - 1], rows.at[:, RING - d, 0, 0], o_s.at[d - 1], o_r.at[d - 1], q_peer[d])

    def d_q(c, d):
        return send(staged.at[c % STAGES, d - 1], rows.at[c, RING - d, pl.ds(1, 3), 0],
                    d_s.at[4 + d, c], d_r.at[4 + d, c], q_peer[d])

    def d_qx(c, d):
        return send(staged_x.at[c % STAGES, d - 1], rows.at[c, RING - d, :, 1],
                    d_s.at[7 + d, c], d_r.at[7 + d, c], q_peer[d])

    def d_twin(c, side, k):
        return send(rows.at[c, k, :, side], rows_x.at[c, :, k, side], l_s.at[side, k, c], l_r.at[side, k, c], twin)

    def h_twin(side, k):
        return send(hid.at[k, :, side], hid_x.at[:, k, side], h_s.at[side, k], h_r.at[side, k], twin)

    def c_q(c, side, d):
        return send(rows.at[c, d, :, side], rows_x.at[c, RING - d, :, side],
                    c_s.at[side, d - 1, c], c_r.at[side, d - 1, c], q_peer[d])

    def c_x(c):
        return send(blocks.at[c, 0], pair_in.at[c], x_s.at[RING, c], x_r.at[RING, c], x_side)

    def c_over(c, d):
        return send(blocks.at[c, 1, d], parts.at[c, d], x_s.at[d, c], x_r.at[d, c], over[d])

    load_g = pltpu.make_async_copy(wg_hbm.at[0, 0], wg, w_sem.at[0])
    load_u = pltpu.make_async_copy(wu_hbm.at[0, 0], wu, w_sem.at[1])
    load_d = pltpu.make_async_copy(
        wd_hbm.at[0, 0, :, pl.ds(pl.multiple_of(core * feats, feats), feats)], wd.at[0], w_sem.at[2])
    give_d = send(wd_hbm.at[0, 0, :, pl.ds(pl.multiple_of((1 - core) * feats, feats), feats)], wd.at[1],
                  wd_s.at[0], wd_r.at[0], twin)

    for c in range(P_AHEAD):
        for d in (1, 3, 2):
            d_p(c, d).start()

    ids = ids_ref[...]
    home = jnp.zeros_like(ids)
    for e in range(experts):
        home = jnp.where(ids == e, place_ref[0, e], home)
    m_index = lax.broadcasted_iota(jnp.int32, (experts, n_tok), 0)
    chosen = jnp.zeros((experts, n_tok), F32)
    weight = jnp.zeros((experts, n_tok), F32)
    for k in range(ids.shape[0]):
        same = home[k:k + 1, :] == m_index
        chosen = chosen + jnp.where(same, 1.0, 0.0)
        weight = weight + jnp.where(same, gates_ref[k:k + 1, :], 0.0)
    earlier = jnp.where(lax.broadcasted_iota(jnp.int32, (n_tok, n_tok), 0)
                        < lax.broadcasted_iota(jnp.int32, (n_tok, n_tok), 1), 1.0, 0.0).astype(BF)
    count = jnp.dot(chosen.astype(BF), earlier, preferred_element_type=F32)
    aux[0, 0, :experts, :] = jnp.where(chosen > 0.5, count, -1.0)
    aux[0, 0, experts:, :] = weight

    a_p = [None] + [send(aux.at[0, 0], aux.at[0, RING - d], aux_s.at[d], aux_r.at[d], p_peer[d])
                    for d in range(1, RING)]
    a_x = send(aux.at[0], aux.at[1], aux_s.at[0], aux_r.at[0], x_side)
    for d in range(1, RING):
        a_p[d].start()

    slot_index = lax.broadcasted_iota(jnp.int32, (CAP, n_tok), 0).astype(F32)

    def table(side, b):
        parts_of = []
        for k in range(RING):
            m = p * step_p + ((q + k) % RING) * step_q + x
            here = aux[side, b, pl.ds(m, 1), :] == slot_index
            pick[side, b, k * CAP:(k + 1) * CAP, :] = jnp.where(here, 1.0, 0.0).astype(BF)
            parts_of.append(jnp.where(here, aux[side, b, pl.ds(experts + m, 1), :], 0.0))
        whole = jnp.concatenate(parts_of, axis=0).T
        top = whole.astype(BF)
        spread[0, side, b] = top
        spread[1, side, b] = (whole - top.astype(F32)).astype(BF)

    table(0, 0)
    for c in range(CHUNKS):
        mine = tok[:, c * width:(c + 1) * width]
        blocks[c, 0, 0] = mine
        if c < X_AHEAD:
            d_x_own(c).start()
        got = jnp.dot(pick[0, 0], mine, preferred_element_type=F32).astype(BF)
        rows[c, 0, 0, 0] = got[:CAP]
        for d in range(1, RING):
            first[d - 1, c] = got[d * CAP:(d + 1) * CAP]
    for d in (2, 1, 3):
        d_first(d).start()
    load_g.start()
    load_u.start()
    load_d.start()
    give_d.start()
    for d in range(1, RING):
        a_p[d].wait_recv()
    a_x.start()

    @pl.loop(1, RING)
    def _(b):
        table(0, b)

    acc_g[...] = jnp.zeros_like(acc_g)
    acc_u[...] = jnp.zeros_like(acc_u)

    def accumulate(c, side):
        own = pl.ds(pl.multiple_of(core * feats + c * width, width), width)
        other = pl.ds(pl.multiple_of((1 - core) * feats + c * width, width), width)

        @pl.loop(0, RING)
        def _(k):
            mine = rows[c, k, :, side].reshape(RING * CAP, width)
            theirs = rows_x[c, k, :, side].reshape(RING * CAP, width)
            acc_g[side, k] += (jnp.dot(mine, wg[own, :], preferred_element_type=F32)
                               + jnp.dot(theirs, wg[other, :], preferred_element_type=F32))
            acc_u[side, k] += (jnp.dot(mine, wu[own, :], preferred_element_type=F32)
                               + jnp.dot(theirs, wu[other, :], preferred_element_type=F32))

    def activate(side):
        for d in range(1, RING):
            pl.semaphore_signal(ready_q.at[side], inc=1, device_id=q_peer[d], device_id_type=MESH)

        for k in range(RING):
            g = acc_g[side, k]
            h = g / (1.0 + jnp.exp(-g)) * acc_u[side, k]
            hid[k, :, side] = h.astype(BF).reshape(RING, CAP, h.shape[-1])
            h_twin(side, k).start()

    def project(c, side):
        @pl.loop(0, RING)
        def _(k):
            mine = hid[k, :, side].reshape(RING * CAP, hid.shape[-1])
            theirs = hid_x[k, :, side].reshape(RING * CAP, hid.shape[-1])
            made = (jnp.dot(mine, wd[0, :, lanes(c)], preferred_element_type=F32)
                    + jnp.dot(theirs, wd[1, :, lanes(c)], preferred_element_type=F32))
            rows[c, k, :, side] = made.astype(BF).reshape(RING, CAP, width)

        for d in (2, 1, 3):
            c_q(c, side, d).start()

    def spread_out(c, side, b):
        got = jnp.concatenate(
            [rows[c, 0, b, side], rows_x[c, 1, b, side], rows_x[c, 2, b, side], rows_x[c, 3, b, side]], axis=0)
        return (jnp.dot(spread[0, side, b], got, preferred_element_type=F32)
                + jnp.dot(spread[1, side, b], got, preferred_element_type=F32))

    def stage(c, run):
        @pl.when((c >= 0) & (c < CHUNKS))
        def _():
            run(c)

    def gather_own(c):
        @pl.when(c + P_AHEAD < CHUNKS)
        def _():
            for d in (1, 3, 2):
                d_p(c + P_AHEAD, d).start()
        for d in (1, 3, 2):
            d_p(c, d).wait_recv()
        d_x(c).start()

        @pl.when(c + X_AHEAD < CHUNKS)
        def _():
            d_x_own(c + X_AHEAD).start()

        @pl.when(c >= STAGES)
        def _():
            for d in range(1, RING):
                d_q(c - STAGES, d).wait_send()

        for b in range(1, RING):
            got = jnp.dot(pick[0, b], blocks[c, 0, b], preferred_element_type=F32).astype(BF)
            rows[c, 0, b, 0] = got[:CAP]
            for d in range(1, RING):
                staged[c % STAGES, d - 1, b - 1] = got[d * CAP:(d + 1) * CAP]
        for d in (2, 1, 3):
            d_q(c, d).start()
        d_twin(c, 0, 0).start()

    def gather_other(c):
        @pl.when(c == 0)
        def _():
            a_x.wait_recv()

            @pl.loop(0, RING)
            def _(b):
                table(1, b)

        d_x_own(c).wait_recv()
        d_x(c).wait_recv()

        @pl.when(c >= STAGES)
        def _():
            for d in range(1, RING):
                d_qx(c - STAGES, d).wait_send()

        for b in range(RING):
            got = jnp.dot(pick[1, b], blocks[c, 1, b], preferred_element_type=F32).astype(BF)
            rows[c, 0, b, 1] = got[:CAP]
            for d in range(1, RING):
                staged_x[c % STAGES, d - 1, b] = got[d * CAP:(d + 1) * CAP]
        for d in (2, 1, 3):
            d_qx(c, d).start()
        d_twin(c, 1, 0).start()

    def share_own(c):
        @pl.when(c == 0)
        def _():
            for d in range(1, RING):
                d_first(d).wait_recv()
        for d in range(1, RING):
            d_q(c, d).wait_recv()
            d_twin(c, 0, RING - d).start()

    def share_other(c):
        for d in range(1, RING):
            d_qx(c, d).wait_recv()
            d_twin(c, 1, RING - d).start()

    def multiply_own(c):
        @pl.when(c == 0)
        def _():
            load_g.wait()
            load_u.wait()
        for k in range(RING):
            d_twin(c, 0, k).wait_recv()
        accumulate(c, 0)

        @pl.when(c == CHUNKS - 1)
        def _():
            activate(0)

    def multiply_other(c):
        for k in range(RING):
            d_twin(c, 1, k).wait_recv()
        accumulate(c, 1)

        @pl.when(c == CHUNKS - 1)
        def _():
            activate(1)

    def project_own(c):
        @pl.when(c == 0)
        def _():
            @pl.loop(0, CHUNKS)
            def _(e):
                for d in range(1, RING):
                    d_p(e, d).wait_send()
                d_x_own(e).wait_send()
                d_x(e).wait_send()
                for k in range(RING):
                    d_twin(e, 0, k).wait_send()
            load_d.wait()
            give_d.wait()
            for k in range(RING):
                h_twin(0, k).wait_recv()
            pl.semaphore_wait(ready_q.at[0], RING - 1)
        project(c, 0)

    def project_other(c):
        @pl.when(c == 0)
        def _():
            @pl.loop(0, CHUNKS)
            def _(e):
                for k in range(RING):
                    d_twin(e, 1, k).wait_send()
            for k in range(RING):
                h_twin(1, k).wait_recv()
            pl.semaphore_wait(ready_q.at[1], RING - 1)
        project(c, 1)

    def add_own(c):
        for d in range(1, RING):
            c_q(c, 0, d).wait_recv()
        for b in range(RING):
            blocks[c, 0, b] = spread_out(c, 0, b).astype(BF)
        c_x(c).start()

    def add_other(c):
        for d in range(1, RING):
            c_q(c, 1, d).wait_recv()
        c_x(c).wait_recv()
        for b in (2, 1, 3, 0):
            total = spread_out(c, 1, b) + pair_in[c, b].astype(F32)
            if b == 0:
                total = total + blocks[c, 1, 0].astype(F32)
            blocks[c, 1, b] = total.astype(BF)
            c_over(c, b).start()

    def finish(c):
        for d in range(RING):
            c_over(c, d).wait_recv()
        total = parts[c, 0].astype(F32) + parts[c, 1].astype(F32)
        total = total + parts[c, 2].astype(F32) + parts[c, 3].astype(F32)
        out[:, lanes(c)] = total.astype(BF)

    @pl.loop(0, 2 * CHUNKS + SHARE + ADD + LAG + 2)
    def _(i):
        j = i - CHUNKS - SHARE - 1
        stage(i, gather_own)
        stage(i - LAG, gather_other)
        stage(j, project_own)
        stage(j - LAG, project_other)
        stage(i - SHARE, share_own)
        stage(i - SHARE - LAG, share_other)
        stage(i - SHARE - 1, multiply_own)
        stage(i - SHARE - LAG - 1, multiply_other)
        stage(j - ADD, add_own)
        stage(j - ADD - LAG, add_other)
        stage(j - ADD - LAG - 1, finish)

    @pl.loop(CHUNKS - STAGES, CHUNKS)
    def _(c):
        for d in range(1, RING):
            d_q(c, d).wait_send()
            d_qx(c, d).wait_send()
    for d in range(1, RING):
        a_p[d].wait_send()
        d_first(d).wait_send()
    a_x.wait_send()
    for side in range(2):
        for k in range(RING):
            h_twin(side, k).wait_send()

    @pl.loop(0, CHUNKS)
    def _(c):
        for d in range(1, RING):
            c_q(c, 0, d).wait_send()
            c_q(c, 1, d).wait_send()
        c_x(c).wait_send()
        for d in range(RING):
            c_over(c, d).wait_send()


def body(tokens, expert_ids, gate_weights, expert_node, w_gate, w_up, w_down):
    own = tokens[0]
    n_tok, feats = own.shape
    width = feats // CHUNKS
    hidden = w_gate.shape[3]
    deep = w_gate.shape[2]
    reach = (2, RING, RING * CAP, hidden)
    vmem = pl.BlockSpec(memory_space=pltpu.VMEM)
    anywhere = pl.BlockSpec(memory_space=pl.ANY)
    dma = pltpu.SemaphoreType.DMA
    held = pltpu.VMEM
    out = pl.pallas_call(
        kernel,
        out_shape=jax.ShapeDtypeStruct((n_tok, feats), BF),
        in_specs=[vmem, vmem, pl.BlockSpec(memory_space=pltpu.SMEM), vmem, anywhere, anywhere, anywhere],
        out_specs=vmem,
        scratch_shapes=[
            held((CHUNKS, 2, RING, n_tok, width), BF),
            held((2, RING, 2 * expert_node.shape[1], n_tok), F32),
            held((2, RING, RING * CAP, n_tok), BF),
            held((2, 2, RING, n_tok, RING * CAP), BF),
            held((RING - 1, CHUNKS, CAP, width), BF),
            held((STAGES, RING - 1, RING - 1, CAP, width), BF),
            held((STAGES, RING - 1, RING, CAP, width), BF),
            held((CHUNKS, RING, RING, 2, CAP, width), BF),
            held((CHUNKS, RING, RING, 2, CAP, width), BF),
            held(reach, F32),
            held(reach, F32),
            held((deep, hidden), BF),
            held((deep, hidden), BF),
            held((2, hidden, feats), BF),
            held((RING, RING, 2, CAP, hidden), BF),
            held((RING, RING, 2, CAP, hidden), BF),
            held((CHUNKS, RING, n_tok, width), BF),
            held((CHUNKS, RING, n_tok, width), BF),
            dma((3,)),
            dma((RING,)),
            dma((RING,)),
            dma((1,)),
            dma((1,)),
            dma((RING - 1,)),
            dma((RING - 1,)),
            dma((11, CHUNKS)),
            dma((11, CHUNKS)),
            dma((2, RING, CHUNKS)),
            dma((2, RING, CHUNKS)),
            dma((2, RING)),
            dma((2, RING)),
            dma((2, RING - 1, CHUNKS)),
            dma((2, RING - 1, CHUNKS)),
            dma((RING + 1, CHUNKS)),
            dma((RING + 1, CHUNKS)),
            pltpu.SemaphoreType.REGULAR((2,)),
        ],
        compiler_params=pltpu.CompilerParams(
            collective_id=0, has_side_effects=True, vmem_limit_bytes=60 * 1024 * 1024),
        name="expert_layer",
    )(expert_ids[0].T, gate_weights[0].T, expert_node, own, w_gate, w_up, w_down)
    return out[None]


def solution(mesh):
    in_specs = (
        P("section", "node", "local"),
        P("section", "node", None),
        P("section", "node", None),
        P("section", None),
        P("section", "node", None, "local"),
        P("section", "node", None, "local"),
        P("section", "node", "local", None),
    )
    out_specs = P("section", "node", "local")
    return jax.shard_map(body, mesh=mesh, in_specs=in_specs, out_specs=out_specs, check_vma=False)
```

```python
import jax
import jax.numpy as jnp
from jax import lax
from jax.experimental import pallas as pl
from jax.experimental.pallas import tpu as pltpu
from jax.sharding import PartitionSpec as P

MESH = pl.DeviceIdType.MESH
BF = jnp.bfloat16
F32 = jnp.float32
RING = 4
CAP = 64
CHUNKS = 8
STAGES = 3
LAG = 2
SHARE = 1
ADD = 2
P_AHEAD = 2
X_AHEAD = 2


def kernel(ids_ref, gates_ref, place_ref, tok, wg_hbm, wu_hbm, wd_hbm, out,
           blocks, aux, pick, spread, first, staged, staged_x, rows, rows_x, acc_g, acc_u, wg, wu, wd, hid, hid_x,
           pair_in, parts,
           w_sem, wd_load, aux_s, aux_r, wd_s, wd_r, o_s, o_r, d_s, d_r, l_s, l_r, h_s, h_r, c_s, c_r, x_s, x_r, ready_q):
    n_tok, feats = tok.shape
    width = feats // CHUNKS
    experts = place_ref.shape[1]
    core = lax.axis_index("local")
    section = lax.axis_index("section")
    node = lax.axis_index("node")
    z, y, x = node // 8, (node // 2) % 4, node % 2
    p = z + core * (y - z)
    q = y + core * (z - y)
    step_p = 8 - 6 * core
    step_q = 2 + 6 * core

    def at_node(dp, dq, dx, segment=section):
        n = ((p + dp) % RING) * step_p + ((q + dq) % RING) * step_q + (x + dx) % 2
        return {"node": n, "local": core, "section": segment}

    p_peer = [None] + [at_node(d, 0, 0) for d in range(1, RING)]
    q_peer = [None] + [at_node(0, d, 0) for d in range(1, RING)]
    x_side = at_node(0, 0, 1)
    twin = {"node": node, "local": 1 - core, "section": section}
    over = [at_node(d, 0, 1, 1 - section) for d in range(RING)]

    def send(src, dst, s, r, to):
        return pltpu.make_async_remote_copy(src_ref=src, dst_ref=dst, send_sem=s, recv_sem=r,
                                            device_id=to, device_id_type=MESH)

    barrier = pltpu.get_barrier_semaphore()
    peers = p_peer[1:] + q_peer[1:] + [x_side, twin] + over
    for peer in peers:
        pl.semaphore_signal(barrier, inc=1, device_id=peer, device_id_type=MESH)
    pl.semaphore_wait(barrier, len(peers))

    def lanes(c):
        return pl.ds(pl.multiple_of(c * width, width), width)

    def d_p(c, d):
        return send(tok.at[:, lanes(c)], blocks.at[c, 0, RING - d], d_s.at[d, c], d_r.at[d, c], p_peer[d])

    def d_x_own(c):
        return send(blocks.at[c, 0, 0], blocks.at[c, 1, 0], d_s.at[0, c], d_r.at[0, c], x_side)

    def d_x(c):
        return send(blocks.at[c, 0, pl.ds(1, 3)], blocks.at[c, 1, pl.ds(1, 3)], d_s.at[4, c], d_r.at[4, c], x_side)

    def d_first(d):
        return send(first.at[d - 1], rows.at[:, RING - d, 0, 0], o_s.at[d - 1], o_r.at[d - 1], q_peer[d])

    def d_q(c, d):
        return send(staged.at[c % STAGES, d - 1], rows.at[c, RING - d, pl.ds(1, 3), 0],
                    d_s.at[4 + d, c], d_r.at[4 + d, c], q_peer[d])

    def d_qx(c, d):
        return send(staged_x.at[c % STAGES, d - 1], rows.at[c, RING - d, :, 1],
                    d_s.at[7 + d, c], d_r.at[7 + d, c], q_peer[d])

    def d_twin(c, side, k):
        return send(rows.at[c, k, :, side], rows_x.at[c, :, k, side], l_s.at[side, k, c], l_r.at[side, k, c], twin)

    def h_twin(side, k):
        return send(hid.at[k, :, side], hid_x.at[:, k, side], h_s.at[side, k], h_r.at[side, k], twin)

    def c_q(c, d):
        return send(rows.at[c, d, :, 0], rows_x.at[c, RING - d, :, 0],
                    c_s.at[0, d - 1, c], c_r.at[0, d - 1, c], q_peer[d])

    def c_q_pair(c, h, d):
        return send(rows.at[c, d, pl.ds(2 * h, 2), 1], rows_x.at[c, RING - d, pl.ds(2 * h, 2), 1],
                    c_s.at[1 + h, d - 1, c], c_r.at[1 + h, d - 1, c], q_peer[d])

    def c_x(c):
        return send(blocks.at[c, 0], pair_in.at[c], x_s.at[RING, c], x_r.at[RING, c], x_side)

    def c_over(c, d):
        return send(blocks.at[c, 1, d], parts.at[c, d], x_s.at[d, c], x_r.at[d, c], over[d])

    hidden = wd_hbm.shape[2]
    own_wd, twin_wd = pl.ds(0, hidden), pl.ds(hidden, hidden)

    def load(c, part, which):
        from_row = ((core + part) % 2) * feats + c * width
        source, held = ((wg_hbm, wg), (wu_hbm, wu))[which]
        return pltpu.make_async_copy(source.at[0, 0, pl.ds(pl.multiple_of(from_row, width), width)],
                                     held.at[c, pl.ds(part * width, width)], w_sem.at[which, part, c])

    load_d = pltpu.make_async_copy(
        wd_hbm.at[0, 0, :, pl.ds(pl.multiple_of(core * feats, feats), feats)], wd.at[own_wd], wd_load.at[0])
    give_d = send(wd_hbm.at[0, 0, :, pl.ds(pl.multiple_of((1 - core) * feats, feats), feats)], wd.at[twin_wd],
                  wd_s.at[0], wd_r.at[0], twin)

    for c in range(P_AHEAD):
        for d in (1, 3, 2):
            d_p(c, d).start()

    ids = ids_ref[...]
    home = jnp.zeros_like(ids)
    for e in range(experts):
        home = jnp.where(ids == e, place_ref[0, e], home)
    m_index = lax.broadcasted_iota(jnp.int32, (experts, n_tok), 0)
    chosen = jnp.zeros((experts, n_tok), F32)
    weight = jnp.zeros((experts, n_tok), F32)
    for k in range(ids.shape[0]):
        same = home[k:k + 1, :] == m_index
        chosen = chosen + jnp.where(same, 1.0, 0.0)
        weight = weight + jnp.where(same, gates_ref[k:k + 1, :], 0.0)
    earlier = jnp.where(lax.broadcasted_iota(jnp.int32, (n_tok, n_tok), 0)
                        < lax.broadcasted_iota(jnp.int32, (n_tok, n_tok), 1), 1.0, 0.0).astype(BF)
    count = jnp.dot(chosen.astype(BF), earlier, preferred_element_type=F32)
    aux[0, 0, :experts, :] = jnp.where(chosen > 0.5, count, -1.0)
    aux[0, 0, experts:, :] = weight

    a_p = [None] + [send(aux.at[0, 0], aux.at[0, RING - d], aux_s.at[d], aux_r.at[d], p_peer[d])
                    for d in range(1, RING)]
    a_x = send(aux.at[0], aux.at[1], aux_s.at[0], aux_r.at[0], x_side)
    for d in range(1, RING):
        a_p[d].start()

    slot_index = lax.broadcasted_iota(jnp.int32, (CAP, n_tok), 0).astype(F32)

    def table(side, b):
        parts_of = []
        for k in range(RING):
            m = p * step_p + ((q + k) % RING) * step_q + x
            here = aux[side, b, pl.ds(m, 1), :] == slot_index
            pick[side, b, k * CAP:(k + 1) * CAP, :] = jnp.where(here, 1.0, 0.0).astype(BF)
            parts_of.append(jnp.where(here, aux[side, b, pl.ds(experts + m, 1), :], 0.0))
        whole = jnp.concatenate(parts_of, axis=0).T
        top = whole.astype(BF)
        spread[side, b, :n_tok, :] = top
        spread[side, b, n_tok:, :] = (whole - top.astype(F32)).astype(BF)

    table(0, 0)
    for c in range(CHUNKS):
        mine = tok[:, c * width:(c + 1) * width]
        blocks[c, 0, 0] = mine
        if c < X_AHEAD:
            d_x_own(c).start()
        got = jnp.dot(pick[0, 0], mine, preferred_element_type=F32).astype(BF)
        rows[c, 0, 0, 0] = got[:CAP]
        for d in range(1, RING):
            first[d - 1, c] = got[d * CAP:(d + 1) * CAP]
    for d in (2, 1, 3):
        d_first(d).start()
    for c in range(CHUNKS):
        for part in range(2):
            for which in range(2):
                load(c, part, which).start()
    load_d.start()
    give_d.start()
    for d in range(1, RING):
        a_p[d].wait_recv()
    a_x.start()

    @pl.loop(1, RING)
    def _(b):
        table(0, b)

    acc_g[...] = jnp.zeros_like(acc_g)
    acc_u[...] = jnp.zeros_like(acc_u)

    def accumulate(c, side):
        many = RING * RING * CAP
        both = jnp.concatenate([rows[c, :, :, side].reshape(many, width),
                                rows_x[c, :, :, side].reshape(many, width)], axis=1)
        for acc, held in ((acc_g, wg), (acc_u, wu)):
            acc[side] += jnp.dot(both, held[c], preferred_element_type=F32).reshape(acc.shape[1:])

    def activate(side):
        for d in range(1, RING):
            pl.semaphore_signal(ready_q.at[side], inc=1, device_id=q_peer[d], device_id_type=MESH)

        for k in range(RING):
            g = acc_g[side, k]
            h = g / (1.0 + jnp.exp(-g)) * acc_u[side, k]
            hid[k, :, side] = h.astype(BF).reshape(RING, CAP, h.shape[-1])
            h_twin(side, k).start()

    def project(c, side):
        many = RING * RING * CAP
        both = jnp.concatenate([hid[:, :, side].reshape(many, hidden),
                                hid_x[:, :, side].reshape(many, hidden)], axis=1)
        made = jnp.dot(both, wd[:, lanes(c)], preferred_element_type=F32)
        rows[c, :, :, side] = made.astype(BF).reshape(RING, RING, CAP, width)

        for d in (2, 1, 3):
            if side == 0:
                c_q(c, d).start()
            else:
                c_q_pair(c, 1, d).start()
        if side == 1:
            for d in (2, 1, 3):
                c_q_pair(c, 0, d).start()

    def spread_out(c, side, b):
        got = jnp.concatenate(
            [rows[c, 0, b, side], rows_x[c, 1, b, side], rows_x[c, 2, b, side], rows_x[c, 3, b, side]], axis=0)
        twice = jnp.dot(spread[side, b], got, preferred_element_type=F32)
        return twice[:n_tok] + twice[n_tok:]

    def stage(c, run):
        @pl.when((c >= 0) & (c < CHUNKS))
        def _():
            run(c)

    def gather_own(c):
        @pl.when(c + P_AHEAD < CHUNKS)
        def _():
            for d in (1, 3, 2):
                d_p(c + P_AHEAD, d).start()
        for d in (1, 3, 2):
            d_p(c, d).wait_recv()
        d_x(c).start()

        @pl.when(c + X_AHEAD < CHUNKS)
        def _():
            d_x_own(c + X_AHEAD).start()

        @pl.when(c >= STAGES)
        def _():
            for d in range(1, RING):
                d_q(c - STAGES, d).wait_send()

        for b in range(1, RING):
            got = jnp.dot(pick[0, b], blocks[c, 0, b], preferred_element_type=F32).astype(BF)
            rows[c, 0, b, 0] = got[:CAP]
            for d in range(1, RING):
                staged[c % STAGES, d - 1, b - 1] = got[d * CAP:(d + 1) * CAP]
        for d in (2, 1, 3):
            d_q(c, d).start()
        d_twin(c, 0, 0).start()

    def gather_other(c):
        @pl.when(c == 0)
        def _():
            a_x.wait_recv()

            @pl.loop(0, RING)
            def _(b):
                table(1, b)

        d_x_own(c).wait_recv()
        d_x(c).wait_recv()

        @pl.when(c >= STAGES)
        def _():
            for d in range(1, RING):
                d_qx(c - STAGES, d).wait_send()

        for b in range(RING):
            got = jnp.dot(pick[1, b], blocks[c, 1, b], preferred_element_type=F32).astype(BF)
            rows[c, 0, b, 1] = got[:CAP]
            for d in range(1, RING):
                staged_x[c % STAGES, d - 1, b] = got[d * CAP:(d + 1) * CAP]
        for d in (2, 1, 3):
            d_qx(c, d).start()
        d_twin(c, 1, 0).start()

    def share_own(c):
        @pl.when(c == 0)
        def _():
            for d in range(1, RING):
                d_first(d).wait_recv()
        for d in range(1, RING):
            d_q(c, d).wait_recv()
            d_twin(c, 0, RING - d).start()

    def share_other(c):
        for d in range(1, RING):
            d_qx(c, d).wait_recv()
            d_twin(c, 1, RING - d).start()

    def multiply_own(c):
        for part in range(2):
            for which in range(2):
                load(c, part, which).wait()
        for k in range(RING):
            d_twin(c, 0, k).wait_recv()
        accumulate(c, 0)

        @pl.when(c == CHUNKS - 1)
        def _():
            activate(0)

    def multiply_other(c):
        for k in range(RING):
            d_twin(c, 1, k).wait_recv()
        accumulate(c, 1)

        @pl.when(c == CHUNKS - 1)
        def _():
            activate(1)

    def project_own(c):
        @pl.when(c == 0)
        def _():
            @pl.loop(0, CHUNKS)
            def _(e):
                for d in range(1, RING):
                    d_p(e, d).wait_send()
                d_x_own(e).wait_send()
                d_x(e).wait_send()
                for k in range(RING):
                    d_twin(e, 0, k).wait_send()
            load_d.wait()
            give_d.wait()
            for k in range(RING):
                h_twin(0, k).wait_recv()
            pl.semaphore_wait(ready_q.at[0], RING - 1)
        project(c, 0)

    def project_other(c):
        @pl.when(c == 0)
        def _():
            @pl.loop(0, CHUNKS)
            def _(e):
                for k in range(RING):
                    d_twin(e, 1, k).wait_send()
            for k in range(RING):
                h_twin(1, k).wait_recv()
            pl.semaphore_wait(ready_q.at[1], RING - 1)
        project(c, 1)

    def add_own(c):
        for d in range(1, RING):
            c_q(c, d).wait_recv()
        for b in range(RING):
            blocks[c, 0, b] = spread_out(c, 0, b).astype(BF)
        c_x(c).start()

    def add_other(c):
        c_x(c).wait_recv()
        for b in (2, 3, 1, 0):
            if b in (2, 1):
                for d in range(1, RING):
                    c_q_pair(c, b // 2, d).wait_recv()
            total = spread_out(c, 1, b) + pair_in[c, b].astype(F32)
            if b == 0:
                total = total + blocks[c, 1, 0].astype(F32)
            blocks[c, 1, b] = total.astype(BF)
            c_over(c, b).start()

    def finish(c):
        for d in range(RING):
            c_over(c, d).wait_recv()
        total = parts[c, 0].astype(F32) + parts[c, 1].astype(F32)
        total = total + parts[c, 2].astype(F32) + parts[c, 3].astype(F32)
        out[:, lanes(c)] = total.astype(BF)

    @pl.loop(0, 2 * CHUNKS + SHARE + ADD + LAG + 2)
    def _(i):
        j = i - CHUNKS - SHARE - 1
        stage(i, gather_own)
        stage(i - LAG, gather_other)
        stage(j, project_own)
        stage(j - LAG, project_other)
        stage(i - SHARE, share_own)
        stage(i - SHARE - LAG, share_other)
        stage(i - SHARE - 1, multiply_own)
        stage(i - SHARE - LAG - 1, multiply_other)
        stage(j - ADD, add_own)
        stage(j - ADD - LAG, add_other)
        stage(j - ADD - LAG - 1, finish)

    @pl.loop(CHUNKS - STAGES, CHUNKS)
    def _(c):
        for d in range(1, RING):
            d_q(c, d).wait_send()
            d_qx(c, d).wait_send()
    for d in range(1, RING):
        a_p[d].wait_send()
        d_first(d).wait_send()
    a_x.wait_send()
    for side in range(2):
        for k in range(RING):
            h_twin(side, k).wait_send()

    @pl.loop(0, CHUNKS)
    def _(c):
        for d in range(1, RING):
            c_q(c, d).wait_send()
            c_q_pair(c, 0, d).wait_send()
            c_q_pair(c, 1, d).wait_send()
        c_x(c).wait_send()
        for d in range(RING):
            c_over(c, d).wait_send()


def body(tokens, expert_ids, gate_weights, expert_node, w_gate, w_up, w_down):
    own = tokens[0]
    n_tok, feats = own.shape
    width = feats // CHUNKS
    hidden = w_gate.shape[3]
    reach = (2, RING, RING * CAP, hidden)
    vmem = pl.BlockSpec(memory_space=pltpu.VMEM)
    anywhere = pl.BlockSpec(memory_space=pl.ANY)
    dma = pltpu.SemaphoreType.DMA
    held = pltpu.VMEM
    out = pl.pallas_call(
        kernel,
        out_shape=jax.ShapeDtypeStruct((n_tok, feats), BF),
        in_specs=[vmem, vmem, pl.BlockSpec(memory_space=pltpu.SMEM), vmem, anywhere, anywhere, anywhere],
        out_specs=vmem,
        scratch_shapes=[
            held((CHUNKS, 2, RING, n_tok, width), BF),
            held((2, RING, 2 * expert_node.shape[1], n_tok), F32),
            held((2, RING, RING * CAP, n_tok), BF),
            held((2, RING, 2 * n_tok, RING * CAP), BF),
            held((RING - 1, CHUNKS, CAP, width), BF),
            held((STAGES, RING - 1, RING - 1, CAP, width), BF),
            held((STAGES, RING - 1, RING, CAP, width), BF),
            held((CHUNKS, RING, RING, 2, CAP, width), BF),
            held((CHUNKS, RING, RING, 2, CAP, width), BF),
            held(reach, F32),
            held(reach, F32),
            held((CHUNKS, 2 * width, hidden), BF),
            held((CHUNKS, 2 * width, hidden), BF),
            held((2 * hidden, feats), BF),
            held((RING, RING, 2, CAP, hidden), BF),
            held((RING, RING, 2, CAP, hidden), BF),
            held((CHUNKS, RING, n_tok, width), BF),
            held((CHUNKS, RING, n_tok, width), BF),
            dma((2, 2, CHUNKS)),
            dma((1,)),
            dma((RING,)),
            dma((RING,)),
            dma((1,)),
            dma((1,)),
            dma((RING - 1,)),
            dma((RING - 1,)),
            dma((11, CHUNKS)),
            dma((11, CHUNKS)),
            dma((2, RING, CHUNKS)),
            dma((2, RING, CHUNKS)),
            dma((2, RING)),
            dma((2, RING)),
            dma((3, RING - 1, CHUNKS)),
            dma((3, RING - 1, CHUNKS)),
            dma((RING + 1, CHUNKS)),
            dma((RING + 1, CHUNKS)),
            pltpu.SemaphoreType.REGULAR((2,)),
        ],
        compiler_params=pltpu.CompilerParams(
            collective_id=0, has_side_effects=True, vmem_limit_bytes=60 * 1024 * 1024),
        name="expert_layer",
    )(expert_ids[0].T, gate_weights[0].T, expert_node, own, w_gate, w_up, w_down)
    return out[None]


def solution(mesh):
    in_specs = (
        P("section", "node", "local"),
        P("section", "node", None),
        P("section", "node", None),
        P("section", None),
        P("section", "node", None, "local"),
        P("section", "node", None, "local"),
        P("section", "node", "local", None),
    )
    out_specs = P("section", "node", "local")
    return jax.shard_map(body, mesh=mesh, in_specs=in_specs, out_specs=out_specs, check_vma=False)
```

```python
import jax
import jax.numpy as jnp
from jax import lax
from jax.experimental import pallas as pl
from jax.experimental.pallas import tpu as pltpu
from jax.sharding import PartitionSpec as P

MESH = pl.DeviceIdType.MESH
BF = jnp.bfloat16
F32 = jnp.float32
RING = 4
CAP = 64
CHUNKS = 8
KEEP = 2
FIRST = 2
STAGES = 3
LAG = 2
SHARE = 1
ADD = 2
P_AHEAD = 2
X_AHEAD = 2


def kernel(ids_ref, gates_ref, place_ref, tok, wg_hbm, wu_hbm, wd_hbm, out,
           blocks, aux, pick, spread, first, staged, staged_x, rows, rows_x, acc_g, acc_u, wg, wu, wd, hid, hid_x,
           pair_in, parts, kept,
           w_sem, wd_load, aux_s, aux_r, wd_s, wd_r, o_s, o_r, d_s, d_r, l_s, l_r, h_s, h_r, c_s, c_r, x_s, x_r, ready_q):
    n_tok, feats = tok.shape
    width = feats // CHUNKS
    experts = place_ref.shape[1]
    core = lax.axis_index("local")
    section = lax.axis_index("section")
    node = lax.axis_index("node")
    z, y, x = node // 8, (node // 2) % 4, node % 2
    p = z + core * (y - z)
    q = y + core * (z - y)
    step_p = 8 - 6 * core
    step_q = 2 + 6 * core

    def at_node(dp, dq, dx, segment=section):
        n = ((p + dp) % RING) * step_p + ((q + dq) % RING) * step_q + (x + dx) % 2
        return {"node": n, "local": core, "section": segment}

    p_peer = [None] + [at_node(d, 0, 0) for d in range(1, RING)]
    q_peer = [None] + [at_node(0, d, 0) for d in range(1, RING)]
    x_side = at_node(0, 0, 1)
    twin = {"node": node, "local": 1 - core, "section": section}
    over = at_node(0, 0, 1, 1 - section)

    def send(src, dst, s, r, to):
        return pltpu.make_async_remote_copy(src_ref=src, dst_ref=dst, send_sem=s, recv_sem=r,
                                            device_id=to, device_id_type=MESH)

    barrier = pltpu.get_barrier_semaphore()
    peers = p_peer[1:] + q_peer[1:] + [x_side, twin, over]
    for peer in peers:
        pl.semaphore_signal(barrier, inc=1, device_id=peer, device_id_type=MESH)
    pl.semaphore_wait(barrier, len(peers))

    def lanes(c):
        return pl.ds(pl.multiple_of(c * width, width), width)

    def d_p(c, d):
        return send(tok.at[:, lanes(c)], blocks.at[c, 0, RING - d], d_s.at[d, c], d_r.at[d, c], p_peer[d])

    def d_x_own(c):
        return send(blocks.at[c, 0, 0], blocks.at[c, 1, 0], d_s.at[0, c], d_r.at[0, c], x_side)

    def d_x(c):
        return send(blocks.at[c, 0, pl.ds(1, 3)], blocks.at[c, 1, pl.ds(1, 3)], d_s.at[4, c], d_r.at[4, c], x_side)

    def d_first(g, d):
        chunks = pl.ds(g * FIRST, FIRST)
        return send(first.at[d - 1, chunks], rows.at[chunks, RING - d, 0, 0],
                    o_s.at[g, d - 1], o_r.at[g, d - 1], q_peer[d])

    def d_q(c, d):
        return send(staged.at[c % STAGES, d - 1], rows.at[c, RING - d, pl.ds(1, 3), 0],
                    d_s.at[4 + d, c], d_r.at[4 + d, c], q_peer[d])

    def d_qx(c, d):
        return send(staged_x.at[c % STAGES, d - 1], rows.at[c, RING - d, :, 1],
                    d_s.at[7 + d, c], d_r.at[7 + d, c], q_peer[d])

    def d_twin(c, side, k):
        return send(rows.at[c, k, :, side], rows_x.at[c, :, k, side], l_s.at[side, k, c], l_r.at[side, k, c], twin)

    def h_twin(side, k):
        return send(hid.at[k, :, side], hid_x.at[:, k, side], h_s.at[side, k], h_r.at[side, k], twin)

    def c_q(c, d):
        return send(rows.at[c, d, :, 0], rows_x.at[c, RING - d, :, 0],
                    c_s.at[0, d - 1, c], c_r.at[0, d - 1, c], q_peer[d])

    def c_q_pair(c, h, d):
        return send(rows.at[c, d, pl.ds(2 * h, 2), 1], rows_x.at[c, RING - d, pl.ds(2 * h, 2), 1],
                    c_s.at[1 + h, d - 1, c], c_r.at[1 + h, d - 1, c], q_peer[d])

    def c_x(c):
        return send(blocks.at[c, 0], pair_in.at[c], x_s.at[RING, c], x_r.at[RING, c], x_side)

    def c_p(c, d):
        return send(blocks.at[c, 1, d], parts.at[c, RING - d - 1], x_s.at[d, c], x_r.at[d, c], p_peer[d])

    def c_over(c):
        return send(blocks.at[c, 1, 0], out.at[:, lanes(c)], x_s.at[0, c], x_r.at[0, c], over)

    hidden = wd_hbm.shape[2]
    own_wd, twin_wd = pl.ds(0, hidden), pl.ds(hidden, hidden)

    def load(c, part, which):
        from_row = ((core + part) % 2) * feats + c * width
        source, held = ((wg_hbm, wg), (wu_hbm, wu))[which]
        return pltpu.make_async_copy(source.at[0, 0, pl.ds(pl.multiple_of(from_row, width), width)],
                                     held.at[c, pl.ds(part * width, width)], w_sem.at[which, part, c])

    load_d = pltpu.make_async_copy(
        wd_hbm.at[0, 0, :, pl.ds(pl.multiple_of(core * feats, feats), feats)], wd.at[own_wd], wd_load.at[0])
    give_d = send(wd_hbm.at[0, 0, :, pl.ds(pl.multiple_of((1 - core) * feats, feats), feats)], wd.at[twin_wd],
                  wd_s.at[0], wd_r.at[0], twin)

    for c in range(P_AHEAD):
        for d in (1, 3, 2):
            d_p(c, d).start()

    ids = ids_ref[...]
    home = jnp.zeros_like(ids)
    for e in range(experts):
        home = jnp.where(ids == e, place_ref[0, e], home)
    m_index = lax.broadcasted_iota(jnp.int32, (experts, n_tok), 0)
    chosen = jnp.zeros((experts, n_tok), F32)
    weight = jnp.zeros((experts, n_tok), F32)
    for k in range(ids.shape[0]):
        same = home[k:k + 1, :] == m_index
        chosen = chosen + jnp.where(same, 1.0, 0.0)
        weight = weight + jnp.where(same, gates_ref[k:k + 1, :], 0.0)
    earlier = jnp.where(lax.broadcasted_iota(jnp.int32, (n_tok, n_tok), 0)
                        < lax.broadcasted_iota(jnp.int32, (n_tok, n_tok), 1), 1.0, 0.0).astype(BF)
    count = jnp.dot(chosen.astype(BF), earlier, preferred_element_type=F32)
    aux[0, 0, :experts, :] = jnp.where(chosen > 0.5, count, -1.0)
    aux[0, 0, experts:, :] = weight

    a_p = [None] + [send(aux.at[0, 0], aux.at[0, RING - d], aux_s.at[d], aux_r.at[d], p_peer[d])
                    for d in range(1, RING)]
    a_x = send(aux.at[0], aux.at[1], aux_s.at[0], aux_r.at[0], x_side)
    for d in range(1, RING):
        a_p[d].start()

    slot_index = lax.broadcasted_iota(jnp.int32, (CAP, n_tok), 0).astype(F32)

    def table(side, b):
        for k in range(RING):
            m = p * step_p + ((q + k) % RING) * step_q + x
            here = aux[side, b, pl.ds(m, 1), :] == slot_index
            pick[side, b, k * CAP:(k + 1) * CAP, :] = jnp.where(here, 1.0, 0.0).astype(BF)

    def spread_table(side, b):
        weights = []
        for k in range(RING):
            m = p * step_p + ((q + k) % RING) * step_q + x
            here = aux[side, b, pl.ds(m, 1), :] == slot_index
            weights.append(jnp.where(here, aux[side, b, pl.ds(experts + m, 1), :], 0.0))
        whole = jnp.concatenate(weights, axis=0).T
        top = whole.astype(BF)
        spread[side, b, :n_tok, :] = top
        spread[side, b, n_tok:, :] = (whole - top.astype(F32)).astype(BF)

    table(0, 0)
    for c in range(CHUNKS):
        mine = tok[:, c * width:(c + 1) * width]
        blocks[c, 0, 0] = mine
        if c < X_AHEAD:
            d_x_own(c).start()
        got = jnp.dot(pick[0, 0], mine, preferred_element_type=F32).astype(BF)
        rows[c, 0, 0, 0] = got[:CAP]
        for d in range(1, RING):
            first[d - 1, c] = got[d * CAP:(d + 1) * CAP]
        if c % FIRST == FIRST - 1:
            for d in (2, 1, 3):
                d_first(c // FIRST, d).start()
    for c in range(CHUNKS):
        for part in range(2):
            for which in range(2):
                load(c, part, which).start()
    load_d.start()
    give_d.start()
    acc_g[...] = jnp.zeros_like(acc_g)
    acc_u[...] = jnp.zeros_like(acc_u)
    for d in range(1, RING):
        a_p[d].wait_recv()
    a_x.start()

    @pl.loop(1, RING)
    def _(b):
        table(0, b)


    def accumulate(c, side):
        many = RING * RING * CAP
        both = jnp.concatenate([rows[c, :, :, side].reshape(many, width),
                                rows_x[c, :, :, side].reshape(many, width)], axis=1)
        for acc, held in ((acc_g, wg), (acc_u, wu)):
            acc[side] += jnp.dot(both, held[c], preferred_element_type=F32).reshape(acc.shape[1:])

    def activate(side):
        for d in range(1, RING):
            pl.semaphore_signal(ready_q.at[side], inc=1, device_id=q_peer[d], device_id_type=MESH)

        for k in range(RING):
            g = acc_g[side, k]
            h = g / (1.0 + jnp.exp(-g)) * acc_u[side, k]
            hid[k, :, side] = h.astype(BF).reshape(RING, CAP, h.shape[-1])
            h_twin(side, k).start()

    def project(c, side):
        many = RING * RING * CAP
        both = jnp.concatenate([hid[:, :, side].reshape(many, hidden),
                                hid_x[:, :, side].reshape(many, hidden)], axis=1)
        made = jnp.dot(both, wd[:, lanes(c)], preferred_element_type=F32)
        rows[c, :, :, side] = made.astype(BF).reshape(RING, RING, CAP, width)

        for d in (2, 1, 3):
            if side == 0:
                c_q(c, d).start()
            else:
                c_q_pair(c, 1, d).start()
        if side == 1:
            for d in (2, 1, 3):
                c_q_pair(c, 0, d).start()

    def spread_out(c, side, b):
        got = jnp.concatenate(
            [rows[c, 0, b, side], rows_x[c, 1, b, side], rows_x[c, 2, b, side], rows_x[c, 3, b, side]], axis=0)
        twice = jnp.dot(spread[side, b], got, preferred_element_type=F32)
        return twice[:n_tok] + twice[n_tok:]

    def stage(c, run):
        @pl.when((c >= 0) & (c < CHUNKS))
        def _():
            run(c)

    def gather_own(c):
        @pl.when(c + P_AHEAD < CHUNKS)
        def _():
            for d in (1, 3, 2):
                d_p(c + P_AHEAD, d).start()
        for d in (1, 3, 2):
            d_p(c, d).wait_recv()
        d_x(c).start()

        @pl.when(c + X_AHEAD < CHUNKS)
        def _():
            d_x_own(c + X_AHEAD).start()

        @pl.when(c >= STAGES)
        def _():
            for d in range(1, RING):
                d_q(c - STAGES, d).wait_send()

        for b in range(1, RING):
            got = jnp.dot(pick[0, b], blocks[c, 0, b], preferred_element_type=F32).astype(BF)
            rows[c, 0, b, 0] = got[:CAP]
            for d in range(1, RING):
                staged[c % STAGES, d - 1, b - 1] = got[d * CAP:(d + 1) * CAP]
        for d in (2, 1, 3):
            d_q(c, d).start()
        d_twin(c, 0, 0).start()

    def gather_other(c):
        @pl.when(c == 0)
        def _():
            a_x.wait_recv()

            @pl.loop(0, RING)
            def _(b):
                table(1, b)

        d_x_own(c).wait_recv()
        d_x(c).wait_recv()

        @pl.when(c >= STAGES)
        def _():
            for d in range(1, RING):
                d_qx(c - STAGES, d).wait_send()

        for b in range(RING):
            got = jnp.dot(pick[1, b], blocks[c, 1, b], preferred_element_type=F32).astype(BF)
            rows[c, 0, b, 1] = got[:CAP]
            for d in range(1, RING):
                staged_x[c % STAGES, d - 1, b] = got[d * CAP:(d + 1) * CAP]
        for d in (2, 1, 3):
            d_qx(c, d).start()
        d_twin(c, 1, 0).start()

    def share_own(c):
        @pl.when(c == 0)
        def _():
            for g in range(CHUNKS // FIRST):
                for d in range(1, RING):
                    d_first(g, d).wait_recv()
        for d in range(1, RING):
            d_q(c, d).wait_recv()
            d_twin(c, 0, RING - d).start()

    def share_other(c):
        for d in range(1, RING):
            d_qx(c, d).wait_recv()
            d_twin(c, 1, RING - d).start()

    def multiply_own(c):
        for part in range(2):
            for which in range(2):
                load(c, part, which).wait()
        for k in range(RING):
            d_twin(c, 0, k).wait_recv()
        accumulate(c, 0)

        @pl.when(c == CHUNKS - 1)
        def _():
            activate(0)

    def multiply_other(c):
        for k in range(RING):
            d_twin(c, 1, k).wait_recv()
        accumulate(c, 1)

        @pl.when(c == CHUNKS - 1)
        def _():
            activate(1)

    def project_own(c):
        @pl.when(c == 0)
        def _():
            @pl.loop(0, CHUNKS)
            def _(e):
                for d in range(1, RING):
                    d_p(e, d).wait_send()
                d_x_own(e).wait_send()
                d_x(e).wait_send()
                for k in range(RING):
                    d_twin(e, 0, k).wait_send()
            load_d.wait()
            give_d.wait()
            for k in range(RING):
                h_twin(0, k).wait_recv()
            pl.semaphore_wait(ready_q.at[0], RING - 1)
        project(c, 0)

    def project_other(c):
        @pl.when(c == 0)
        def _():
            @pl.loop(0, CHUNKS)
            def _(e):
                for k in range(RING):
                    d_twin(e, 1, k).wait_send()
            for k in range(RING):
                h_twin(1, k).wait_recv()
            pl.semaphore_wait(ready_q.at[1], RING - 1)
        project(c, 1)

    def add_own(c):
        for d in range(1, RING):
            c_q(c, d).wait_recv()
        for b in range(RING):
            blocks[c, 0, b] = spread_out(c, 0, b).astype(BF)
        c_x(c).start()

    def add_other(c):
        c_x(c).wait_recv()
        for b in (2, 3, 1, 0):
            if b in (2, 1):
                for d in range(1, RING):
                    c_q_pair(c, b // 2, d).wait_recv()
            total = spread_out(c, 1, b) + pair_in[c, b].astype(F32)
            if b == 0:
                kept[c % KEEP] = total + blocks[c, 1, 0].astype(F32)
            else:
                blocks[c, 1, b] = total.astype(BF)
                c_p(c, b).start()

    def finish(c):
        for d in range(1, RING):
            c_p(c, d).wait_recv()
        total = kept[c % KEEP] + parts[c, 0].astype(F32)
        total = total + parts[c, 1].astype(F32) + parts[c, 2].astype(F32)
        blocks[c, 1, 0] = total.astype(BF)
        c_over(c).start()

    @pl.loop(0, 2 * CHUNKS + SHARE + ADD + LAG + 2)
    def _(i):
        j = i - CHUNKS - SHARE - 1
        stage(i, gather_own)
        stage(i - LAG, gather_other)
        stage(j, project_own)
        stage(j - LAG, project_other)
        stage(i - SHARE, share_own)
        stage(i - SHARE - LAG, share_other)
        stage(i - SHARE - 1, multiply_own)
        stage(i - SHARE - LAG - 1, multiply_other)
        stage(j - ADD, add_own)
        stage(j - ADD - LAG, add_other)
        stage(j - ADD - LAG - 1, finish)

        @pl.when((i > LAG) & (i <= LAG + RING))
        def _():
            spread_table(0, i - LAG - 1)
            spread_table(1, i - LAG - 1)

    @pl.loop(CHUNKS - STAGES, CHUNKS)
    def _(c):
        for d in range(1, RING):
            d_q(c, d).wait_send()
            d_qx(c, d).wait_send()
    for d in range(1, RING):
        a_p[d].wait_send()
        for g in range(CHUNKS // FIRST):
            d_first(g, d).wait_send()
    a_x.wait_send()
    for side in range(2):
        for k in range(RING):
            h_twin(side, k).wait_send()

    @pl.loop(0, CHUNKS)
    def _(c):
        for d in range(1, RING):
            c_q(c, d).wait_send()
            c_q_pair(c, 0, d).wait_send()
            c_q_pair(c, 1, d).wait_send()
        c_x(c).wait_send()
        for d in range(1, RING):
            c_p(c, d).wait_send()
        c_over(c).wait()


def body(tokens, expert_ids, gate_weights, expert_node, w_gate, w_up, w_down):
    own = tokens[0]
    n_tok, feats = own.shape
    width = feats // CHUNKS
    hidden = w_gate.shape[3]
    reach = (2, RING, RING * CAP, hidden)
    vmem = pl.BlockSpec(memory_space=pltpu.VMEM)
    anywhere = pl.BlockSpec(memory_space=pl.ANY)
    dma = pltpu.SemaphoreType.DMA
    held = pltpu.VMEM
    out = pl.pallas_call(
        kernel,
        out_shape=jax.ShapeDtypeStruct((n_tok, feats), BF),
        in_specs=[vmem, vmem, pl.BlockSpec(memory_space=pltpu.SMEM), vmem, anywhere, anywhere, anywhere],
        out_specs=anywhere,
        scratch_shapes=[
            held((CHUNKS, 2, RING, n_tok, width), BF),
            held((2, RING, 2 * expert_node.shape[1], n_tok), F32),
            held((2, RING, RING * CAP, n_tok), BF),
            held((2, RING, 2 * n_tok, RING * CAP), BF),
            held((RING - 1, CHUNKS, CAP, width), BF),
            held((STAGES, RING - 1, RING - 1, CAP, width), BF),
            held((STAGES, RING - 1, RING, CAP, width), BF),
            held((CHUNKS, RING, RING, 2, CAP, width), BF),
            held((CHUNKS, RING, RING, 2, CAP, width), BF),
            held(reach, F32),
            held(reach, F32),
            held((CHUNKS, 2 * width, hidden), BF),
            held((CHUNKS, 2 * width, hidden), BF),
            held((2 * hidden, feats), BF),
            held((RING, RING, 2, CAP, hidden), BF),
            held((RING, RING, 2, CAP, hidden), BF),
            held((CHUNKS, RING, n_tok, width), BF),
            held((CHUNKS, RING - 1, n_tok, width), BF),
            held((KEEP, n_tok, width), F32),
            dma((2, 2, CHUNKS)),
            dma((1,)),
            dma((RING,)),
            dma((RING,)),
            dma((1,)),
            dma((1,)),
            dma((CHUNKS // FIRST, RING - 1)),
            dma((CHUNKS // FIRST, RING - 1)),
            dma((11, CHUNKS)),
            dma((11, CHUNKS)),
            dma((2, RING, CHUNKS)),
            dma((2, RING, CHUNKS)),
            dma((2, RING)),
            dma((2, RING)),
            dma((3, RING - 1, CHUNKS)),
            dma((3, RING - 1, CHUNKS)),
            dma((RING + 1, CHUNKS)),
            dma((RING + 1, CHUNKS)),
            pltpu.SemaphoreType.REGULAR((2,)),
        ],
        compiler_params=pltpu.CompilerParams(
            collective_id=0, has_side_effects=True, vmem_limit_bytes=60 * 1024 * 1024),
        name="expert_layer",
    )(expert_ids[0].T, gate_weights[0].T, expert_node, own, w_gate, w_up, w_down)
    return out[None]


def solution(mesh):
    in_specs = (
        P("section", "node", "local"),
        P("section", "node", None),
        P("section", "node", None),
        P("section", None),
        P("section", "node", None, "local"),
        P("section", "node", None, "local"),
        P("section", "node", "local", None),
    )
    out_specs = P("section", "node", "local")
    return jax.shard_map(body, mesh=mesh, in_specs=in_specs, out_specs=out_specs, check_vma=False)
```
